32 devices in a mesh: seq: 8 (over z, x), mp: 4 (over y, core).
Axes of the slice: x: 2, y: 2, z: 4, core: 2. Of those that a mesh axis runs over, the one named last changes fastest.
Arguments:
- tokens: bfloat16 [4096, 2048], P('mp', 'seq'), may hold values from -24 to 24
- packing: int32 [2048], replicated, may hold values from 0 to 2047, as said below
- norm_gain: float32 [4096], replicated, may hold values from 0.5 to 1.5
- w_value: bfloat16 [4096, 4096], P('seq', 'mp'), may hold values from -0.09375 to 0.09375
- w_gate: bfloat16 [4096, 4096], P('seq', 'mp'), may hold values from -0.09375 to 0.09375
- filters: bfloat16 [4096, 256], P('mp'), may hold values from -3 to 3
- skip_gain: float32 [4096], P('mp'), may hold values from -1 to 1
- lengths: int32 [4], replicated, may hold values from 1 to 4, 8 in all
Outputs:
- mixed: bfloat16 [4096, 2048], P('mp', 'seq')
The draws below stay inside these ranges and needn't reach their ends.
Inputs may be any that keep to these rules, and one draw needn't show every extreme that they name: Each of 0 to 2047 appears once. Of the 256 corpus rows j with the same j // 256, at most 64 have the same packing[j] // 256, and in every draw some group reaches 64.
All inputs are finite; a program needn't handle non-finite values.
Results may differ from the reference program's by a relative error of at most 0.0052.
Values may be sent and summed in bfloat16 or wider, within the bound.
No kernel may reach another device: no remote copies, remote signals or barrier semaphores. Data moves between devices by JAX's collectives and lax.ppermute only.
A program may use at most 128 MiB of HBM per device.

```python
import math
import jax
import jax.numpy as jnp
import numpy as np
from jax import lax

D = 4096
TAPS = 256
TOK_DEV = 256
TOKENS = 2048
BLOCKS = 8
DOCS = 4
MOST = 4


def draw_tokens(key, part):
    key_base, key_rows, key_cols = jax.random.split(key, 3)
    base = jnp.clip(jax.random.normal(key_base, (D, TOKENS), jnp.float32), -4.0, 4.0)
    col_scale = jnp.exp(jax.random.uniform(key_cols, (D, 1), jnp.float32, math.log(0.3), math.log(3.0)))
    row_scale = jnp.exp(jax.random.uniform(key_rows, (1, TOKENS), jnp.float32, math.log(0.5), math.log(2.0)))
    return (base * col_scale * row_scale).astype(jnp.bfloat16)


def draw_filters(key, part):
    key_noise, key_rate = jax.random.split(key, 2)
    decay_rate = jnp.exp(jax.random.uniform(key_rate, (D, 1), jnp.float32, math.log(0.64 / TAPS), math.log(10.0 / TAPS)))
    noise = jnp.clip(jax.random.normal(key_noise, (D, TAPS), jnp.float32), -3.0, 3.0)
    tap_index = jnp.arange(TAPS, dtype=jnp.float32)[None, :]
    envelope = jnp.exp(-decay_rate * tap_index) * jnp.sqrt(2.0 * decay_rate)
    return (noise * envelope).astype(jnp.bfloat16)


def draw_packing(key, part):
    shards = TOKENS // TOK_DEV
    mean_count = TOK_DEV // shards
    key_delta, key_order, key_owner, key_rows = jax.random.split(key, 4)
    half_count = shards // 2
    deltas = jax.random.randint(key_delta, (half_count,), 0, mean_count + 1)
    deltas = deltas.at[0].set(mean_count)
    profile = jnp.concatenate([mean_count + deltas, mean_count - deltas])
    profile = jax.random.permutation(key_order, profile)
    sources = jnp.arange(shards)[:, None]
    owners = jnp.arange(shards)[None, :]
    counts = profile[(owners - sources) % shards]
    ends = jnp.cumsum(counts, axis=1)
    slot_ids = jnp.arange(TOK_DEV)
    dest_owner = jnp.sum((ends[:, None, :] <= slot_ids[None, :, None]).astype(jnp.int32), axis=2)
    firsts = ends - counts
    slot_rank = slot_ids[None, :] - jnp.take_along_axis(firsts, dest_owner, axis=1)
    offsets = jnp.cumsum(counts, axis=0) - counts
    within = jnp.take_along_axis(offsets, dest_owner, axis=1) + slot_rank
    owner_keys = jax.random.split(key_owner, shards)
    owner_perms = jax.vmap(lambda one_key: jax.random.permutation(one_key, TOK_DEV))(owner_keys)
    spots = owner_perms[dest_owner, within]
    slot_dest = dest_owner * TOK_DEV + spots
    row_keys = jax.random.split(key_rows, shards)
    row_perms = jax.vmap(lambda one_key: jax.random.permutation(one_key, TOK_DEV))(row_keys)
    dest = jnp.take_along_axis(slot_dest, row_perms, axis=1)
    return dest.reshape(TOKENS).astype(jnp.int32)


def level_of(key, shape, cuts, smallest, largest):
    def one(position, parts):
        steps = jax.random.uniform(jax.random.fold_in(jax.random.fold_in(key, 6), position), (parts,), jnp.float32, smallest / len(cuts), largest / len(cuts))
        return jnp.repeat(jnp.exp(steps), shape[position] // parts).reshape((-1,) + (1,) * (len(shape) - position - 1))

    level = one(*cuts[0])
    for cut in cuts[1:]:
        level = level * one(*cut)
    return level


def split_up(number_of, total, limit, skew):
    portions = [(1 << 20) // math.isqrt(grade ** skew) + 1 for grade in range(2, number_of + 1)]
    surplus, given = total - limit - (number_of - 1), [1] * (number_of - 1)
    while surplus > 0:
        candidates = [i for i in range(number_of - 1) if given[i] < limit]
        pool, left = sum([portions[i] for i in candidates]), surplus
        for i in candidates:
            addition = min(limit - given[i], max(1, left * portions[i] // pool), surplus)
            given[i] = given[i] + addition
            surplus = surplus - addition
    return np.array([limit] + given)


def uneven(stream_key, count, total, reach, skew):
    if count == 2:
        one = jax.random.randint(stream_key, (), max(1, total - reach), min(reach, total - 1) + 1)
        return jnp.stack([one, total - one])
    sizes = jnp.asarray(split_up(count, total, reach, skew), jnp.int32)
    couples = (count - 1) // 2
    giver, receiver = sizes[1:1 + 2 * couples:2], sizes[2:2 + 2 * couples:2]
    slack = jnp.minimum(giver - 1, reach - receiver)
    passed = jax.random.randint(jax.random.fold_in(stream_key, 1), (couples,), 0, 1 << 20) % (slack + 1)
    sizes = sizes.at[1:1 + 2 * couples:2].set(giver - passed).at[2:2 + 2 * couples:2].set(receiver + passed)
    return sizes[jax.random.permutation(jax.random.fold_in(stream_key, 2), count)]


def scatter_about(stream_key, extent, deviation, bound, cuts=(), kind=jnp.bfloat16):
    gain = level_of(stream_key, extent, cuts, -0.22, 0.18) if cuts else 1.0
    array = jax.random.normal(stream_key, extent, jnp.float32) * deviation * gain
    return jnp.minimum(jnp.maximum(array, -bound), bound).astype(kind)


def setup_inputs(seed: int = 0) -> dict:
    arg_keys = jax.random.split(jax.random.key(seed), 9)
    tokens = draw_tokens(jax.random.fold_in(arg_keys[8], 71), 0)
    packing = draw_packing(jax.random.fold_in(arg_keys[8], 71), 0)
    norm_gain = jnp.clip(1.0 + 0.1 * jax.random.normal(arg_keys[2], (D,), jnp.float32), 0.5, 1.5)
    w_value = scatter_about(arg_keys[3], (D, D), D ** -0.5, 0.09375, ((0, 8), (1, 4)))
    w_gate = scatter_about(arg_keys[4], (D, D), D ** -0.5, 0.09375, ((0, 8), (1, 4)))
    filters = draw_filters(jax.random.fold_in(arg_keys[8], 71), 0)
    skip_gain = jnp.clip(jax.random.uniform(arg_keys[6], (D,), jnp.float32, -1.0, 1.0) * level_of(arg_keys[6], (D,), ((0, 4),), -0.4, 0.0), -1.0, 1.0)
    lengths = uneven(arg_keys[7], DOCS, BLOCKS, MOST, 2).astype(jnp.int32)
    return dict(tokens=tokens, packing=packing, norm_gain=norm_gain, w_value=w_value, w_gate=w_gate, filters=filters, skip_gain=skip_gain, lengths=lengths)


epsilon = 1e-05

def toeplitz(filter_taps):
    chan_count, tap_count = filter_taps.shape
    padding = jnp.zeros((chan_count, tap_count), filter_taps.dtype)
    line_row = jnp.concatenate([padding, filter_taps[:, ::-1], padding], axis=1)
    tiled = jnp.tile(line_row, (1, tap_count))[:, :tap_count * (3 * tap_count - 1)]
    return tiled.reshape(chan_count, tap_count, 3 * tap_count - 1)[:, :, tap_count - 1:3 * tap_count - 1]

def doc_flags(lengths, first_block, block_count, dtype):
    starts = jnp.cumsum(lengths, dtype=jnp.int32) - lengths
    block_index = first_block + jnp.arange(block_count, dtype=jnp.int32)
    is_start = jnp.any(block_index[:, None] == starts[None, :], axis=1)
    return jnp.where(is_start, 0.0, 1.0).astype(dtype)

def band_product(values, prior_rim, filter_taps, link_flags):
    chan_count, seq_length = values.shape
    tap_count = filter_taps.shape[1]
    block_count = seq_length // tap_count
    group_size = math.gcd(chan_count, 64)
    groups = chan_count // group_size

    def one_group(group_args):
        part_values, part_rim, part_taps = group_args
        blocks = part_values.reshape(group_size, block_count, tap_count)
        earlier = jnp.concatenate([part_rim[:, None, :], blocks[:, :-1, :]], axis=1)
        earlier = earlier * link_flags[None, :, None]
        joined = jnp.concatenate([earlier, blocks], axis=2)
        banded = jnp.einsum('cpq,cbq->cbp', toeplitz(part_taps), joined, preferred_element_type=jnp.float32)
        return banded.reshape(group_size, seq_length)
    result = lax.map(one_group, (values.reshape(groups, group_size, seq_length), prior_rim.reshape(groups, group_size, tap_count), filter_taps.reshape(groups, group_size, tap_count)))
    return result.reshape(chan_count, seq_length)

def reference(tokens, packing, norm_gain, w_value, w_gate, filters, skip_gain, lengths):
    packed = jnp.zeros_like(tokens).at[:, packing].set(tokens)
    widened = packed.astype(jnp.float32)
    inv_scale = lax.rsqrt(lax.optimization_barrier(jnp.mean(widened * widened, axis=0, keepdims=True)) + epsilon)
    normed = (widened * inv_scale * norm_gain[:, None]).astype(jnp.bfloat16)
    value_part = jnp.dot(w_value.T, normed, preferred_element_type=jnp.float32).astype(jnp.bfloat16)
    gate_part = jnp.dot(w_gate.T, normed, preferred_element_type=jnp.float32).astype(jnp.bfloat16)
    link_flags = doc_flags(lengths, 0, BLOCKS, jnp.float32)
    prior_rim = jnp.zeros((D, TAPS), jnp.float32)
    value_wide = value_part.astype(jnp.float32)
    banded = band_product(value_wide, prior_rim, filters.astype(jnp.float32), link_flags)
    mixed_band = (banded + skip_gain[:, None] * value_wide).astype(jnp.bfloat16)
    mixed_band = lax.optimization_barrier(mixed_band)
    gate_wide = lax.optimization_barrier(gate_part).astype(jnp.float32)
    return (widened + gate_wide * mixed_band.astype(jnp.float32)).astype(jnp.bfloat16)
```

```python
import functools
import math

import jax
import jax.numpy as jnp
from jax import lax
from jax.experimental import pallas as pl
from jax.experimental.pallas import tpu as pltpu
from jax.sharding import PartitionSpec as P

epsilon = 1e-05
AXES = ("seq", "mp")
LANES = 128
SUBLANES = 8
VMEM = pl.BlockSpec(memory_space=pltpu.VMEM)
SMEM = pl.BlockSpec(memory_space=pltpu.SMEM)
PARAMS = pltpu.CompilerParams(vmem_limit_bytes=48 * 1024 * 1024)


def toeplitz(filter_taps):
    chan_count, tap_count = filter_taps.shape
    padding = jnp.zeros((chan_count, tap_count), filter_taps.dtype)
    line_row = jnp.concatenate([padding, filter_taps[:, ::-1], padding], axis=1)
    tiled = jnp.tile(line_row, (1, tap_count))[:, : tap_count * (3 * tap_count - 1)]
    return tiled.reshape(chan_count, tap_count, 3 * tap_count - 1)[
        :, :, tap_count - 1 : 3 * tap_count - 1
    ]


def doc_flags(lengths, block_count, dtype):
    starts = jnp.cumsum(lengths, dtype=jnp.int32) - lengths
    block_index = jnp.arange(block_count, dtype=jnp.int32)
    is_start = jnp.any(block_index[:, None] == starts[None, :], axis=1)
    return jnp.where(is_start, 0.0, 1.0).astype(dtype)


def band_product(values, prior_rim, filter_taps, link_flags):
    chan_count, seq_length = values.shape
    tap_count = filter_taps.shape[1]
    block_count = seq_length // tap_count
    group_size = math.gcd(chan_count, 64)
    groups = chan_count // group_size

    def one_group(group_args):
        part_values, part_rim, part_taps = group_args
        blocks = part_values.reshape(group_size, block_count, tap_count)
        earlier = jnp.concatenate([part_rim[:, None, :], blocks[:, :-1, :]], axis=1)
        earlier = earlier * link_flags[None, :, None]
        joined = jnp.concatenate([earlier, blocks], axis=2)
        banded = jnp.einsum(
            "cpq,cbq->cbp", toeplitz(part_taps), joined, preferred_element_type=jnp.float32
        )
        return banded.reshape(group_size, seq_length)

    result = lax.map(
        one_group,
        (
            values.reshape(groups, group_size, seq_length),
            prior_rim.reshape(groups, group_size, tap_count),
            filter_taps.reshape(groups, group_size, tap_count),
        ),
    )
    return result.reshape(chan_count, seq_length)


def project_all(all_features, norm_gain, weight_pair):
    widened = all_features.astype(jnp.float32)
    inv_scale = lax.rsqrt(jnp.mean(widened * widened, axis=0, keepdims=True) + epsilon)
    normed = (widened * inv_scale * norm_gain[:, None]).astype(jnp.bfloat16)
    contract = (((0,), (0,)), ((), ()))
    value_part = lax.dot_general(
        weight_pair[0], normed, contract, preferred_element_type=jnp.float32
    ).astype(jnp.bfloat16)
    gate_part = lax.dot_general(
        weight_pair[1], normed, contract, preferred_element_type=jnp.float32
    ).astype(jnp.bfloat16)
    return (value_part, gate_part)


def on_device(tokens, packing, norm_gain, w_value, w_gate, filters, skip_gain, lengths):
    row_count = tokens.shape[1]
    shards = lax.axis_size("seq")
    my_index = lax.axis_index("seq")
    all_count = packing.shape[0]
    tap_count = filters.shape[1]
    chan_count = tokens.shape[0] // shards
    weight_pair = (
        lax.all_gather(w_value, "seq", axis=0, tiled=True),
        lax.all_gather(w_gate, "seq", axis=0, tiled=True),
    )
    inverse = (
        jnp.zeros((all_count,), jnp.int32).at[packing].set(jnp.arange(all_count, dtype=jnp.int32))
    )
    chan_taps = lax.dynamic_slice_in_dim(filters, my_index * chan_count, chan_count, 0)
    chan_skip = lax.dynamic_slice_in_dim(skip_gain, my_index * chan_count, chan_count, 0)
    slot_cap = 2 * (row_count // shards)
    own_packing = lax.dynamic_slice_in_dim(packing, my_index * row_count, row_count)
    dest_owner = own_packing // row_count
    onehot = (dest_owner[:, None] == jnp.arange(shards, dtype=jnp.int32)[None, :]).astype(jnp.int32)
    slot_rank = jnp.sum((jnp.cumsum(onehot, axis=0, dtype=jnp.int32) - onehot) * onehot, axis=1)
    slot_index = dest_owner * slot_cap + slot_rank
    send_buffer = (
        jnp.zeros((tokens.shape[0], shards * slot_cap), jnp.bfloat16).at[:, slot_index].set(tokens)
    )
    received = lax.all_to_all(send_buffer, "seq", split_axis=1, concat_axis=1, tiled=True)
    my_sources = lax.dynamic_slice_in_dim(inverse, my_index * row_count, row_count)
    to_me = (packing // row_count == my_index).astype(jnp.int32).reshape(shards, row_count)
    arrival_rank = (jnp.cumsum(to_me, axis=1, dtype=jnp.int32) - to_me).reshape(all_count)
    packed = received[:, my_sources // row_count * slot_cap + arrival_rank[my_sources]]
    all_features = lax.all_gather(packed, "mp", axis=0, tiled=True)
    value_part, gate_part = project_all(all_features, norm_gain, weight_pair)
    value_chan = lax.all_to_all(value_part, "seq", split_axis=0, concat_axis=1, tiled=True)
    link_flags = doc_flags(lengths, all_count // tap_count, jnp.bfloat16)
    prior_rim = jnp.zeros((chan_count, tap_count), jnp.bfloat16)
    banded = band_product(value_chan, prior_rim, chan_taps, link_flags)
    chan_band = (banded + chan_skip[:, None] * value_chan.astype(jnp.float32)).astype(jnp.bfloat16)
    mixed_band = lax.all_to_all(chan_band, "seq", split_axis=1, concat_axis=0, tiled=True)
    mixed_band = lax.optimization_barrier(mixed_band)
    gate_wide = lax.optimization_barrier(gate_part).astype(jnp.float32)
    return (packed.astype(jnp.float32) + gate_wide * mixed_band.astype(jnp.float32)).astype(
        jnp.bfloat16
    )


def pack_kernel(line, place_ref, value_ref, gate_ref, *out_refs):
    height, columns = value_ref.shape
    width = columns // (2 * line)
    z = place_ref[0]
    for d in range(line):
        target = lax.rem(z + d, line)
        for half in range(2):
            first = pl.multiple_of(half * (columns // 2) + target * width, width)
            for which, ref in enumerate((value_ref, gate_ref)):
                out_refs[d][half, which] = ref[:, pl.ds(first, width)].T


def pack_weights(place, w_value, w_gate, line):
    height, columns = w_value.shape
    width = columns // (2 * line)
    return pl.pallas_call(
        functools.partial(pack_kernel, line),
        out_shape=[jax.ShapeDtypeStruct((2, 2, width, height), w_value.dtype)] * line,
        in_specs=[SMEM, VMEM, VMEM],
        out_specs=[VMEM] * line,
        compiler_params=PARAMS,
        cost_estimate=pl.CostEstimate(
            flops=0, bytes_accessed=8 * height * columns, transcendentals=0
        ),
    )(place, w_value, w_gate)


def project_kernel(pick_ref, weight_ref, inv_ref, gain_ref, *refs):
    parts = len(refs) - 2
    mine_ref, other_ref = refs[parts:]
    x = pick_ref[parts]
    inv_row = inv_ref[...]
    rows = mine_ref.shape[0]
    height = weight_ref.shape[-1]
    mine = jnp.zeros(mine_ref.shape, jnp.float32)
    other = jnp.zeros(mine_ref.shape, jnp.float32)
    for part in range(parts):
        pick = pick_ref[part]
        scaled = refs[part][...].astype(jnp.float32) * inv_row * gain_ref[part]
        scaled = scaled.astype(jnp.bfloat16)
        near = weight_ref[pick, x].reshape(rows, height)
        far = weight_ref[pick, 1 - x].reshape(rows, height)
        mine += jnp.dot(near, scaled, preferred_element_type=jnp.float32)
        other += jnp.dot(far, scaled, preferred_element_type=jnp.float32)
    mine_ref[...] = mine
    other_ref[...] = other.astype(jnp.bfloat16)


def project(picks, weights, inv_row, gain_columns, blocks):
    line, _, _, width, height = weights.shape
    count = blocks[0].shape[1]
    out = (2 * width, count)
    return pl.pallas_call(
        project_kernel,
        out_shape=[
            jax.ShapeDtypeStruct(out, jnp.float32),
            jax.ShapeDtypeStruct(out, jnp.bfloat16),
        ],
        in_specs=[SMEM] + [VMEM] * (3 + len(blocks)),
        out_specs=[VMEM, VMEM],
        compiler_params=PARAMS,
        cost_estimate=pl.CostEstimate(
            flops=8 * width * height * count * len(blocks),
            bytes_accessed=weights.size * 2 + 2 * height * count * len(blocks),
            transcendentals=0,
        ),
    )(picks, weights, inv_row, gain_columns, *blocks)


def mix_kernel(slots, taps_blocks, flag_ref, place_ref, taps_ref, skip_ref, *refs):
    mine_refs, theirs_refs, token_refs = refs[:slots], refs[slots : 2 * slots], refs[2 * slots : 3 * slots]
    out_ref = refs[3 * slots]
    whole, band = refs[3 * slots + 1], refs[3 * slots + 2]
    shifted = refs[3 * slots + 3 :]
    chan = taps_ref.shape[0]
    count = mine_refs[0].shape[1]
    pieces = shifted[0].shape[0] // chan
    total = pieces * LANES
    for slot in range(slots):
        summed = (mine_refs[slot][...] + theirs_refs[slot][...].astype(jnp.float32)).astype(jnp.bfloat16)
        stacked = jnp.concatenate([summed, token_refs[slot][...]], axis=0)
        spot = lax.broadcasted_iota(jnp.int32, (count, total), 1)
        onehot = (place_ref[slot] == spot).astype(jnp.float32).astype(jnp.bfloat16)
        moved = jnp.dot(stacked, onehot, preferred_element_type=jnp.float32)
        if slot == 0:
            whole[...] = moved
        else:
            whole[...] += moved
    for piece in range(pieces):
        for back in range(taps_blocks + 1):
            rows = pl.ds(piece * chan, chan)
            if back > piece:
                shifted[back][rows, :] = jnp.zeros((chan, LANES), jnp.float32)
                continue
            first = (piece - back) * LANES
            part = whole[0:chan, first : first + LANES]
            if back > piece % taps_blocks:
                part = part * flag_ref[piece // taps_blocks]
            shifted[back][rows, :] = part
    column = lax.broadcasted_iota(jnp.int32, (LANES, LANES), 1)
    row = lax.broadcasted_iota(jnp.int32, (LANES, LANES), 0)
    later = column >= row

    zero = jnp.zeros((LANES, LANES), jnp.float32)

    def one(group, carry):
        base = pl.multiple_of(group * SUBLANES, SUBLANES)
        group_taps = taps_ref[pl.ds(base, SUBLANES), :]
        for member in range(SUBLANES):
            turned = [zero]
            for block in range(taps_blocks):
                line_row = group_taps[member : member + 1, block * LANES : (block + 1) * LANES]
                square = jnp.broadcast_to(line_row, (LANES, LANES))
                turned.append(pltpu.roll(square, 0, 1, stride=1, stride_axis=0))
            turned.append(zero)
            rows = pl.ds(base + member, pieces, stride=chan)
            tiles, inputs = [], []
            for back in range(taps_blocks + 1):
                tiles.append(jnp.where(later, turned[back + 1], turned[back]).astype(jnp.bfloat16))
                inputs.append(shifted[back][rows, :].astype(jnp.bfloat16))
            band[rows, :] = jnp.dot(
                jnp.concatenate(inputs, axis=1),
                jnp.concatenate(tiles, axis=0),
                preferred_element_type=jnp.float32,
            )
        return carry

    lax.fori_loop(0, chan // SUBLANES, one, 0)
    skip = skip_ref[...]
    wide = out_ref.shape[2] // LANES
    for piece in range(pieces):
        lanes = slice(piece * LANES, (piece + 1) * LANES)
        rows = pl.ds(piece * chan, chan)
        z = (band[rows, :] + skip * whole[0:chan, lanes]).astype(jnp.bfloat16).astype(jnp.float32)
        mixed = whole[2 * chan : 3 * chan, lanes] + whole[chan : 2 * chan, lanes] * z
        inner = (piece % wide) * LANES
        out_ref[piece // wide, :, inner : inner + LANES] = mixed.astype(jnp.bfloat16)


def mix(flags, places, taps, skip, mine, theirs, tokens, shards):
    slots = len(mine)
    chan, tap_count = taps.shape
    total = slots * mine[0].shape[1]
    taps_blocks = tap_count // LANES
    return pl.pallas_call(
        functools.partial(mix_kernel, slots, taps_blocks),
        out_shape=jax.ShapeDtypeStruct((shards, chan, total // shards), jnp.bfloat16),
        in_specs=[SMEM] + [VMEM] * (3 + 3 * slots),
        out_specs=VMEM,
        scratch_shapes=[
            pltpu.VMEM((3 * chan, total), jnp.float32),
            pltpu.VMEM((total // LANES * chan, LANES), jnp.float32),
        ]
        + [pltpu.VMEM((total // LANES * chan, LANES), jnp.float32)] * (taps_blocks + 1),
        compiler_params=PARAMS,
        cost_estimate=pl.CostEstimate(
            flops=6 * chan * total * total, bytes_accessed=16 * chan * total, transcendentals=0
        ),
    )(flags, places, taps, skip, *mine, *theirs, *tokens)


def on_device_line(tokens, packing, norm_gain, w_value, w_gate, filters, skip_gain, lengths):
    shards, groups = lax.axis_size("seq"), lax.axis_size("mp")
    line = shards // 2
    s, m = lax.axis_index("seq"), lax.axis_index("mp")
    z, x = s // 2, s % 2
    features, row_count = tokens.shape
    half = features // 2
    total_rows = packing.shape[0]
    pair_rows = 2 * row_count
    width = features // shards

    def send(array, target):
        pairs = []
        for zz in range(line):
            for xx in range(2):
                for mm in range(groups):
                    to = target(zz, xx, mm)
                    if to is not None:
                        pairs.append(
                            (
                                (zz * 2 + xx) * groups + mm,
                                (to[0] * 2 + to[1]) * groups + to[2],
                            )
                        )
        return lax.ppermute(array, AXES, pairs)

    def across(array):
        return send(array, lambda zz, xx, mm: (zz, 1 - xx, mm))

    keep = lax.dynamic_slice_in_dim(tokens, x * half, half, 0)
    give = lax.dynamic_slice_in_dim(tokens, (1 - x) * half, half, 0)
    got = across(give)
    place = jnp.stack([z]).astype(jnp.int32)
    packed_weights = pack_weights(place, w_value, w_gate, line)
    weights = [packed_weights[0]]
    for d in range(1, line):
        weights.append(send(packed_weights[d], lambda zz, xx, mm, d=d: ((zz + d) % line, xx, mm)))
    weights = jnp.stack(weights)

    own = jnp.where(
        x == 0, jnp.concatenate([keep, got], axis=1), jnp.concatenate([got, keep], axis=1)
    )
    up, down = [own], [own]
    for step in range(1, line):
        up.append(
            send(
                up[-1],
                lambda zz, xx, mm: (zz + 1, xx, mm) if step - 1 <= zz < line - 1 else None,
            )
        )
        down.append(
            send(
                down[-1],
                lambda zz, xx, mm: (zz - 1, xx, mm) if 0 < zz <= line - step else None,
            )
        )
    order = [sorted(range(line), key=lambda other: (abs(other - zz), other)) for zz in range(line)]
    slots = []
    for j in range(line):
        chosen = None
        for zz in range(line):
            other = order[zz][j]
            array = up[zz - other] if other <= zz else down[other - zz]
            chosen = array if chosen is None or array is chosen else jnp.where(z == zz, array, chosen)
        slots.append(chosen)
    slot_pair = jnp.asarray(order, jnp.int32)[z]

    widened = tokens.astype(jnp.float32)
    squares = jnp.sum(widened * widened, axis=0)
    spread = lax.dynamic_update_slice_in_dim(
        jnp.zeros((total_rows,), jnp.float32), squares, s * row_count, 0
    )
    mean = lax.psum(spread, AXES) / (features * groups)
    inv_scale = lax.rsqrt(mean + epsilon)

    gain_blocks = norm_gain.reshape(groups, 2, half)[:, x]
    offsets = range(groups)
    owners = [m ^ o for o in offsets]
    picks = jnp.stack([lax.rem(z - owner + line, line) for owner in owners] + [x]).astype(jnp.int32)
    gains = jnp.stack([gain_blocks[owner] for owner in owners])[:, :, None]

    def to_owner(array, o):
        return send(array, lambda zz, xx, mm: (zz, xx, mm ^ o))

    row_blocks = inv_scale.reshape(line, 1, pair_rows)
    pack_blocks = packing.reshape(line, pair_rows, 1)
    mine, theirs, kept, places = [], [], [], []
    for j in range(line):
        own_block = slots[j]
        blocks = [own_block]
        while len(blocks) < groups:
            step = groups // 2 // len(blocks)
            blocks = blocks + [to_owner(b, step) for b in blocks]
        offset_order = [0]
        while len(offset_order) < groups:
            step = groups // 2 // len(offset_order)
            offset_order = offset_order + [o ^ step for o in offset_order]
        blocks = [blocks[offset_order.index(o)] for o in offsets]
        near, far = project(picks, weights, row_blocks[slot_pair[j]], gains, blocks)
        mine.append(near)
        theirs.append(across(far))
        kept.append(lax.dynamic_slice_in_dim(own_block, z * width, width, 0))
        places.append(pack_blocks[slot_pair[j]])

    first = x * half + z * width
    taps = lax.dynamic_slice_in_dim(filters, first, width, 0).astype(jnp.float32)
    skip = lax.dynamic_slice_in_dim(skip_gain, first, width, 0)[:, None]
    flags = doc_flags(lengths, total_rows // filters.shape[1], jnp.float32)
    mixed = mix(flags, jnp.stack(places), taps, skip, mine, theirs, kept, shards)
    mixed = lax.all_to_all(mixed, "seq", split_axis=0, concat_axis=0, tiled=True)
    mixed = mixed.reshape(line, 2, width, row_count).transpose(1, 0, 2, 3)
    return mixed.reshape(features, row_count)


def solution(mesh):
    placed = (P("mp", "seq"), P(), P(), P("seq", "mp"), P("seq", "mp"), P("mp", None), P("mp"), P())
    shards, groups = mesh.shape["seq"], mesh.shape["mp"]

    def whole(*args):
        tokens, w_value, filters = args[0], args[3], args[5]
        moves_tokens = (
            tokens.shape[1] <= w_value.shape[1]
            and shards == 2 * groups
            and groups & (groups - 1) == 0
            and tokens.shape[0] % (LANES * shards * groups) == 0
            and filters.shape[1] % LANES == 0
            and tokens.shape[1] // shards % filters.shape[1] == 0
        )
        body = on_device_line if moves_tokens else on_device
        return jax.shard_map(
            body, mesh=mesh, in_specs=placed, out_specs=P("mp", "seq"), check_vma=False
        )(*args)

    return whole
```

```python
import functools
import math

import jax
import jax.numpy as jnp
from jax import lax
from jax.experimental import pallas as pl
from jax.experimental.pallas import tpu as pltpu
from jax.sharding import PartitionSpec as P

epsilon = 1e-05
AXES = ("seq", "mp")
LANES = 128
SUBLANES = 8
EXTRA = 2 * SUBLANES
VMEM = pl.BlockSpec(memory_space=pltpu.VMEM)
ANY = pl.BlockSpec(memory_space=pl.ANY)
SMEM = pl.BlockSpec(memory_space=pltpu.SMEM)
PARAMS = pltpu.CompilerParams(vmem_limit_bytes=16 * 1024 * 1024)


def toeplitz(filter_taps):
    chan_count, tap_count = filter_taps.shape
    padding = jnp.zeros((chan_count, tap_count), filter_taps.dtype)
    line_row = jnp.concatenate([padding, filter_taps[:, ::-1], padding], axis=1)
    tiled = jnp.tile(line_row, (1, tap_count))[:, : tap_count * (3 * tap_count - 1)]
    return tiled.reshape(chan_count, tap_count, 3 * tap_count - 1)[
        :, :, tap_count - 1 : 3 * tap_count - 1
    ]


def doc_flags(lengths, block_count, dtype):
    starts = jnp.cumsum(lengths, dtype=jnp.int32) - lengths
    block_index = jnp.arange(block_count, dtype=jnp.int32)
    is_start = jnp.any(block_index[:, None] == starts[None, :], axis=1)
    return jnp.where(is_start, 0.0, 1.0).astype(dtype)


def band_product(values, prior_rim, filter_taps, link_flags):
    chan_count, seq_length = values.shape
    tap_count = filter_taps.shape[1]
    block_count = seq_length // tap_count
    group_size = math.gcd(chan_count, 64)
    groups = chan_count // group_size

    def one_group(group_args):
        part_values, part_rim, part_taps = group_args
        blocks = part_values.reshape(group_size, block_count, tap_count)
        earlier = jnp.concatenate([part_rim[:, None, :], blocks[:, :-1, :]], axis=1)
        earlier = earlier * link_flags[None, :, None]
        joined = jnp.concatenate([earlier, blocks], axis=2)
        banded = jnp.einsum(
            "cpq,cbq->cbp", toeplitz(part_taps), joined, preferred_element_type=jnp.float32
        )
        return banded.reshape(group_size, seq_length)

    result = lax.map(
        one_group,
        (
            values.reshape(groups, group_size, seq_length),
            prior_rim.reshape(groups, group_size, tap_count),
            filter_taps.reshape(groups, group_size, tap_count),
        ),
    )
    return result.reshape(chan_count, seq_length)


def project_all(all_features, norm_gain, weight_pair):
    widened = all_features.astype(jnp.float32)
    inv_scale = lax.rsqrt(jnp.mean(widened * widened, axis=0, keepdims=True) + epsilon)
    normed = (widened * inv_scale * norm_gain[:, None]).astype(jnp.bfloat16)
    contract = (((0,), (0,)), ((), ()))
    value_part = lax.dot_general(
        weight_pair[0], normed, contract, preferred_element_type=jnp.float32
    ).astype(jnp.bfloat16)
    gate_part = lax.dot_general(
        weight_pair[1], normed, contract, preferred_element_type=jnp.float32
    ).astype(jnp.bfloat16)
    return (value_part, gate_part)


def on_device(tokens, packing, norm_gain, w_value, w_gate, filters, skip_gain, lengths):
    row_count = tokens.shape[1]
    shards = lax.axis_size("seq")
    my_index = lax.axis_index("seq")
    all_count = packing.shape[0]
    tap_count = filters.shape[1]
    chan_count = tokens.shape[0] // shards
    weight_pair = (
        lax.all_gather(w_value, "seq", axis=0, tiled=True),
        lax.all_gather(w_gate, "seq", axis=0, tiled=True),
    )
    inverse = (
        jnp.zeros((all_count,), jnp.int32).at[packing].set(jnp.arange(all_count, dtype=jnp.int32))
    )
    chan_taps = lax.dynamic_slice_in_dim(filters, my_index * chan_count, chan_count, 0)
    chan_skip = lax.dynamic_slice_in_dim(skip_gain, my_index * chan_count, chan_count, 0)
    slot_cap = 2 * (row_count // shards)
    own_packing = lax.dynamic_slice_in_dim(packing, my_index * row_count, row_count)
    dest_owner = own_packing // row_count
    onehot = (dest_owner[:, None] == jnp.arange(shards, dtype=jnp.int32)[None, :]).astype(jnp.int32)
    slot_rank = jnp.sum((jnp.cumsum(onehot, axis=0, dtype=jnp.int32) - onehot) * onehot, axis=1)
    slot_index = dest_owner * slot_cap + slot_rank
    send_buffer = (
        jnp.zeros((tokens.shape[0], shards * slot_cap), jnp.bfloat16).at[:, slot_index].set(tokens)
    )
    received = lax.all_to_all(send_buffer, "seq", split_axis=1, concat_axis=1, tiled=True)
    my_sources = lax.dynamic_slice_in_dim(inverse, my_index * row_count, row_count)
    to_me = (packing // row_count == my_index).astype(jnp.int32).reshape(shards, row_count)
    arrival_rank = (jnp.cumsum(to_me, axis=1, dtype=jnp.int32) - to_me).reshape(all_count)
    packed = received[:, my_sources // row_count * slot_cap + arrival_rank[my_sources]]
    all_features = lax.all_gather(packed, "mp", axis=0, tiled=True)
    value_part, gate_part = project_all(all_features, norm_gain, weight_pair)
    value_chan = lax.all_to_all(value_part, "seq", split_axis=0, concat_axis=1, tiled=True)
    link_flags = doc_flags(lengths, all_count // tap_count, jnp.bfloat16)
    prior_rim = jnp.zeros((chan_count, tap_count), jnp.bfloat16)
    banded = band_product(value_chan, prior_rim, chan_taps, link_flags)
    chan_band = (banded + chan_skip[:, None] * value_chan.astype(jnp.float32)).astype(jnp.bfloat16)
    mixed_band = lax.all_to_all(chan_band, "seq", split_axis=1, concat_axis=0, tiled=True)
    mixed_band = lax.optimization_barrier(mixed_band)
    gate_wide = lax.optimization_barrier(gate_part).astype(jnp.float32)
    return (packed.astype(jnp.float32) + gate_wide * mixed_band.astype(jnp.float32)).astype(
        jnp.bfloat16
    )


def extend_kernel(token_ref, out_ref):
    features, count = token_ref.shape
    widened = token_ref[...].astype(jnp.float32)
    rest = jnp.sum(widened * widened, axis=0, keepdims=True)
    terms = []
    for _ in range(3):
        term = rest.astype(jnp.bfloat16).astype(jnp.float32)
        terms.append(term)
        rest = rest - term
    row = lax.broadcasted_iota(jnp.int32, (EXTRA, count), 0)
    extra = jnp.zeros(row.shape, jnp.float32)
    for i, term in enumerate(terms):
        extra = jnp.where(row == i, term, extra)
    out_ref[0:features, :] = token_ref[...]
    out_ref[features : features + EXTRA, :] = extra.astype(jnp.bfloat16)


def extend(tokens):
    features, count = tokens.shape
    return pl.pallas_call(
        extend_kernel,
        out_shape=jax.ShapeDtypeStruct((features + EXTRA, count), tokens.dtype),
        in_specs=[VMEM],
        out_specs=VMEM,
        compiler_params=PARAMS,
        cost_estimate=pl.CostEstimate(
            flops=2 * features * count, bytes_accessed=4 * features * count, transcendentals=0
        ),
    )(tokens)


def halve_kernel(x_ref, *refs):
    arrays, (keep_ref, give_ref) = refs[:-2], refs[-2:]
    features = arrays[0].shape[0] - EXTRA
    half = features // 2
    x = x_ref[0]
    for number, ref in enumerate(arrays):
        first = number * (half + EXTRA)
        for out_ref, which in ((keep_ref, x), (give_ref, 1 - x)):
            rows = pl.ds(pl.multiple_of(which * half, half), half)
            out_ref[first : first + half, :] = ref[rows, :]
            out_ref[first + half : first + half + EXTRA, :] = ref[features : features + EXTRA, :]


def halve(x, arrays):
    tall, count = arrays[0].shape
    half = (tall - EXTRA) // 2
    out = jax.ShapeDtypeStruct(((half + EXTRA) * len(arrays), count), arrays[0].dtype)
    return pl.pallas_call(
        halve_kernel,
        out_shape=[out, out],
        in_specs=[SMEM] + [VMEM] * len(arrays),
        out_specs=[VMEM, VMEM],
        compiler_params=PARAMS,
        cost_estimate=pl.CostEstimate(
            flops=0, bytes_accessed=4 * tall * count * len(arrays), transcendentals=0
        ),
    )(x, *arrays)


def pack_kernel(after_ref, *refs):
    out_ref = refs[-1]
    line, _, _, width, _ = out_ref.shape
    for which, ref in enumerate(refs[:-1]):
        for target in range(line):
            for half in range(2):
                first = (half * line + target) * width
                out_ref[target, which, half] = ref[:, first : first + width].T


def pack_weights(after, weights, line):
    height, columns = weights[0].shape
    out = (line, len(weights), 2, columns // (2 * line), height)
    return pl.pallas_call(
        pack_kernel,
        out_shape=jax.ShapeDtypeStruct(out, weights[0].dtype),
        in_specs=[ANY] + [VMEM] * len(weights),
        out_specs=VMEM,
        compiler_params=PARAMS,
        cost_estimate=pl.CostEstimate(
            flops=0, bytes_accessed=4 * height * columns * len(weights), transcendentals=0
        ),
    )(after, *weights)


def scale_kernel(height, pick_ref, gain_ref, *refs):
    arrays, out_ref = refs[:-1], refs[-1]
    parts = out_ref.shape[0]
    tall = height + EXTRA
    blocks = [
        ref.at[first : first + tall] for ref in arrays for first in range(0, ref.shape[0], tall)
    ]
    each = len(blocks) // parts
    count = out_ref.shape[2] // each
    slots = each // 2 if each > 1 else 1
    features = 2 * height * parts
    gain_columns = gain_ref[...].T
    for number in range(each):
        slot, half = number % slots, number // slots
        first = (slot * (each // slots) + half) * count
        squares = jnp.zeros((1, count), jnp.float32)
        for block in blocks[number::each]:
            terms = block[height:tall, :].astype(jnp.float32)
            squares += jnp.sum(terms, axis=0, keepdims=True)
        inv_row = lax.rsqrt(squares / features + epsilon)
        for part in range(parts):
            scaled = blocks[part * each + number][0:height, :].astype(jnp.float32) * inv_row
            scaled = (scaled * gain_columns[:, part : part + 1]).astype(jnp.bfloat16)
            out_ref[pick_ref[part], :, first : first + count] = scaled


def scale(picks, gains, height, arrays):
    parts = picks.shape[0]
    count = arrays[0].shape[1]
    each = sum(array.shape[0] for array in arrays) // (height + EXTRA) // parts
    return pl.pallas_call(
        functools.partial(scale_kernel, height),
        out_shape=jax.ShapeDtypeStruct((parts, height, count * each), jnp.bfloat16),
        in_specs=[SMEM] + [VMEM] * (1 + len(arrays)),
        out_specs=VMEM,
        compiler_params=PARAMS,
        cost_estimate=pl.CostEstimate(
            flops=2 * parts * height * count * each,
            bytes_accessed=4 * parts * height * count * each,
            transcendentals=0,
        ),
    )(picks, gains, *arrays)


def project_kernel(number, starts, row_count, x_ref, weight_ref, *refs):
    mine_ref, other_ref = refs[-2:]
    x = x_ref[0]
    first = 0
    for ref, far in zip(refs[:-2], starts):
        parts, _, count = ref.shape
        for begin in range(0, count, 2 * row_count):
            columns = slice(begin, min(begin + 2 * row_count, count))
            wide = columns.stop - begin
            mine = jnp.zeros((mine_ref.shape[0], wide), jnp.float32)
            other = jnp.zeros((mine_ref.shape[0], wide), jnp.float32)
            for part in range(parts):
                block = ref[part, :, columns]
                for which, is_mine in ((x, True), (1 - x, False)):
                    result = jnp.dot(
                        weight_ref[part, number, which], block, preferred_element_type=jnp.float32
                    )
                    mine, other = (mine + result, other) if is_mine else (mine, other + result)
            mine_ref[:, first + begin : first + begin + wide] = mine
            other = other.astype(jnp.bfloat16)
            if wide > row_count:
                other = jnp.concatenate([other[:, row_count:], other[:, :row_count]], axis=1)
            other_ref[:, far + begin : far + begin + wide] = other
        first += count


def project(x, weights, number, normed, row_count, starts=None):
    line, _, _, width, height = weights.shape
    counts = [some.shape[2] for some in normed]
    starts = starts or [sum(counts[:i]) for i in range(len(counts))]
    out = (width, sum(counts))
    return pl.pallas_call(
        functools.partial(project_kernel, number, starts, row_count),
        out_shape=[
            jax.ShapeDtypeStruct(out, jnp.float32),
            jax.ShapeDtypeStruct(out, jnp.bfloat16),
        ],
        in_specs=[SMEM] + [VMEM] * (1 + len(normed)),
        out_specs=[VMEM] * 2,
        compiler_params=PARAMS,
        cost_estimate=pl.CostEstimate(
            flops=4 * width * height * out[1] * line,
            bytes_accessed=weights.size + 2 * height * out[1] * line,
            transcendentals=0,
        ),
    )(x, weights, *normed)


def column_of(row):
    tall = jnp.broadcast_to(row.astype(jnp.float32), (SUBLANES, row.shape[1])).T
    return tall[:, 0:1].astype(row.dtype)


def at_places(array, place_row, total):
    spot = lax.broadcasted_iota(jnp.int32, (array.shape[1], total), 1)
    onehot = (column_of(place_row) == spot).astype(jnp.float32).astype(jnp.bfloat16)
    return jnp.dot(array, onehot, preferred_element_type=jnp.float32)


def with_tokens(first, tall, summed, token_refs):
    chan = summed.shape[0]
    first = pl.multiple_of(first, chan)
    tokens = []
    for kept_ref, got_ref in zip(token_refs[::2], token_refs[1::2]):
        for start in range(0, kept_ref.shape[0], tall):
            tokens += [ref[pl.ds(first + start, chan), :] for ref in (kept_ref, got_ref)]
    return jnp.concatenate([summed, jnp.concatenate(tokens, axis=1)], axis=0)


def place_kernel(tall, many, first_ref, mine_ref, theirs_ref, place_ref, *refs):
    tokens, before, out_ref = refs[:many], refs[many:-1], refs[-1]
    count = place_ref.shape[1]
    summed = mine_ref[:, :count] + theirs_ref[:, :count].astype(jnp.float32)
    summed = summed.astype(jnp.bfloat16)
    if tokens:
        summed = with_tokens(first_ref[0], tall, summed, tokens)
    moved = at_places(summed, place_ref[...], out_ref.shape[1])
    for ref in before:
        moved += ref[...].astype(jnp.float32)
    out_ref[...] = moved.astype(jnp.bfloat16)


def place(first, total, mine, theirs, places, tall=0, tokens=(), before=()):
    chan, count = mine.shape[0], places.shape[1]
    return pl.pallas_call(
        functools.partial(place_kernel, tall, len(tokens)),
        out_shape=jax.ShapeDtypeStruct((2 * chan if tokens else chan, total), jnp.bfloat16),
        in_specs=[SMEM] + [VMEM] * (3 + len(tokens) + len(before)),
        out_specs=VMEM,
        compiler_params=PARAMS,
        cost_estimate=pl.CostEstimate(
            flops=2 * chan * total * count, bytes_accessed=8 * chan * total, transcendentals=0
        ),
    )(first, mine, theirs, places, *tokens, *before)


def band_kernel(
    taps_blocks, tall, flag_ref, first_ref, taps_ref, skip_ref, early_ref, mine_ref, theirs_ref,
    last_mine_ref, last_theirs_ref, place_ref, *refs
):
    shifted = refs[-taps_blocks - 1 :]
    out_ref, packed_ref, whole, band = refs[-taps_blocks - 5 : -taps_blocks - 1]
    chan = taps_ref.shape[0]
    total = whole.shape[1]
    pieces = total // LANES
    cut = mine_ref.shape[1] - last_mine_ref.shape[1]
    mine = jnp.concatenate([mine_ref[:, cut:], last_mine_ref[...]], axis=1)
    theirs = jnp.concatenate([last_theirs_ref[...], theirs_ref[:, cut:]], axis=1)
    summed = (mine + theirs.astype(jnp.float32)).astype(jnp.bfloat16)
    summed = with_tokens(first_ref[0], tall, summed, refs[: -taps_blocks - 5])
    moved = at_places(summed, place_ref[...], total) + early_ref[...].astype(jnp.float32)
    whole[...] = moved[0:chan]
    packed_ref[...] = moved[chan : 2 * chan].astype(jnp.bfloat16)
    for piece in range(pieces):
        for back in range(taps_blocks + 1):
            rows = pl.ds(piece * chan, chan)
            if back > piece:
                shifted[back][rows, :] = jnp.zeros((chan, LANES), jnp.float32)
                continue
            first = (piece - back) * LANES
            part = whole[:, first : first + LANES]
            if back > piece % taps_blocks:
                part = part * flag_ref[piece // taps_blocks]
            shifted[back][rows, :] = part
    column = lax.broadcasted_iota(jnp.int32, (LANES, LANES), 1)
    row = lax.broadcasted_iota(jnp.int32, (LANES, LANES), 0)
    later = column >= row
    zero = jnp.zeros((LANES, LANES), jnp.float32)

    def one(group, carry):
        base = pl.multiple_of(group * SUBLANES, SUBLANES)
        group_taps = taps_ref[pl.ds(base, SUBLANES), :]
        for member in range(SUBLANES):
            turned = [zero]
            for block in range(taps_blocks):
                line_row = group_taps[member : member + 1, block * LANES : (block + 1) * LANES]
                square = jnp.broadcast_to(line_row, (LANES, LANES))
                turned.append(pltpu.roll(square, 0, 1, stride=1, stride_axis=0))
            turned.append(zero)
            rows = pl.ds(base + member, pieces, stride=chan)
            tiles, inputs = [], []
            for back in range(taps_blocks + 1):
                tiles.append(jnp.where(later, turned[back + 1], turned[back]).astype(jnp.bfloat16))
                inputs.append(shifted[back][rows, :].astype(jnp.bfloat16))
            band[rows, :] = jnp.dot(
                jnp.concatenate(inputs, axis=1),
                jnp.concatenate(tiles, axis=0),
                preferred_element_type=jnp.float32,
            )
        return carry

    lax.fori_loop(0, chan // SUBLANES, one, 0)
    skip = column_of(skip_ref[...])
    for piece in range(pieces):
        lanes = slice(piece * LANES, (piece + 1) * LANES)
        rows = pl.ds(piece * chan, chan)
        out_ref[:, lanes] = (band[rows, :] + skip * whole[:, lanes]).astype(jnp.bfloat16)


def band_of(flags, first, taps, skip, early, late, last, places, tall, tokens):
    chan, tap_count = taps.shape
    total = early.shape[1]
    taps_blocks = tap_count // LANES
    tower = (total // LANES * chan, LANES)
    out = jax.ShapeDtypeStruct((chan, total), jnp.bfloat16)
    return pl.pallas_call(
        functools.partial(band_kernel, taps_blocks, tall),
        out_shape=[out, out],
        in_specs=[SMEM, SMEM] + [VMEM] * (8 + len(tokens)),
        out_specs=[VMEM, VMEM],
        scratch_shapes=[pltpu.VMEM((chan, total), jnp.float32)]
        + [pltpu.VMEM(tower, jnp.float32)] * (taps_blocks + 2),
        compiler_params=PARAMS,
        cost_estimate=pl.CostEstimate(
            flops=3 * chan * total * total, bytes_accessed=16 * chan * total, transcendentals=0
        ),
    )(flags, first, taps, skip, early, *late, *last, places, *tokens)


def mix_kernel(z_ref, packed_ref, early_ref, mine_ref, theirs_ref, place_ref, out_ref):
    summed = (mine_ref[...] + theirs_ref[...].astype(jnp.float32)).astype(jnp.bfloat16)
    gate = at_places(summed, place_ref[...], z_ref.shape[1]) + early_ref[...].astype(jnp.float32)
    mixed = packed_ref[...].astype(jnp.float32) + gate * z_ref[...].astype(jnp.float32)
    mixed = mixed.astype(jnp.bfloat16)
    wide = out_ref.shape[2]
    for owner in range(out_ref.shape[0]):
        out_ref[owner] = mixed[:, owner * wide : (owner + 1) * wide]


def mix(z, packed, early, mine, theirs, places, shards):
    chan, total = z.shape
    return pl.pallas_call(
        mix_kernel,
        out_shape=jax.ShapeDtypeStruct((shards, chan, total // shards), jnp.bfloat16),
        in_specs=[VMEM] * 6,
        out_specs=VMEM,
        compiler_params=PARAMS,
        cost_estimate=pl.CostEstimate(
            flops=chan * total * total, bytes_accessed=16 * chan * total, transcendentals=0
        ),
    )(z, packed, early, mine, theirs, places)


def on_device_line(tokens, packing, norm_gain, w_value, w_gate, filters, skip_gain, lengths):
    shards, groups = lax.axis_size("seq"), lax.axis_size("mp")
    line = shards // 2
    s, m = lax.axis_index("seq"), lax.axis_index("mp")
    z, x = s // 2, s % 2
    features, row_count = tokens.shape
    half = features // 2
    total_rows = packing.shape[0]
    width = features // shards

    def number(zz, xx, mm):
        return (zz * 2 + xx) * groups + mm

    def send(array, target):
        pairs = []
        for zz in range(line):
            for xx in range(2):
                for mm in range(groups):
                    to = target(zz, xx, mm)
                    if to is not None:
                        pairs.append((number(zz, xx, mm), number(*to)))
        return lax.ppermute(array, AXES, pairs)

    def across(array):
        return send(array, lambda zz, xx, mm: (zz, 1 - xx, mm))

    def to_owner(array, o):
        return send(array, lambda zz, xx, mm: (zz, xx, mm ^ o))

    columns = [[number(zz, xx, mm) for zz in range(line)] for xx in range(2) for mm in range(groups)]

    def along_line(array):
        return lax.all_to_all(
            array, AXES, split_axis=0, concat_axis=0, tiled=True, axis_index_groups=columns
        )

    def to_pair(array, o):
        return send(array, lambda zz, xx, mm: (zz ^ o, xx, mm))

    slot_pair = jnp.stack([z ^ o for o in range(line)])
    far_owner, near_owner, far_pair, near_pair = groups // 2, groups // 4, line // 2, line // 4
    owners = jnp.stack([m ^ o for o in (0, far_owner, near_owner, far_owner ^ near_owner)])
    which = x[None].astype(jnp.int32)
    picks = owners.astype(jnp.int32)
    gains = norm_gain.reshape(groups, 2, half)[:, x][owners]
    gains = jnp.pad(gains, ((0, -groups % SUBLANES), (0, 0)))
    places = packing.reshape(line, 2, row_count)[slot_pair]
    places = jnp.stack([places[:, x], places[:, 1 - x]], axis=1).reshape(1, total_rows)
    first = x * half + z * width
    taps = lax.dynamic_slice_in_dim(filters, first, width, 0).astype(jnp.float32)
    skip = lax.dynamic_slice_in_dim(skip_gain, first, width, 0)[None]
    flags = doc_flags(lengths, total_rows // filters.shape[1], jnp.float32)
    row_first = (z * width)[None].astype(jnp.int32)
    tall = half + EXTRA
    wide = 2 * row_count

    def projected(number, some, starts=None):
        return project(which, weights, number, some, row_count, starts)

    def scaled(arrays):
        return scale(picks, gains, half, arrays)

    def to_near(arrays):
        stacked = jnp.concatenate(arrays, axis=0) if len(arrays) > 1 else arrays[0]
        return to_owner(stacked, near_owner)

    def tie(*arrays):
        return lax.optimization_barrier(arrays)

    extended = extend(tokens)
    kept0, give0 = halve(which, [extended])
    by_far, by_near = to_pair(extended, far_pair), to_pair(extended, near_pair)
    got0, kept0_far = across(give0), to_owner(kept0, far_owner)
    got0_far = to_owner(got0, far_owner)
    packed_weights = pack_weights(give0, [w_value, w_gate], line)
    small = picks, gains, taps, skip, flags, row_first, places, which
    by_both = to_pair(by_far, near_pair)
    by_far, by_near, got0, kept0_far, got0_far, small, packed_weights = tie(
        by_far, by_near, got0, kept0_far, got0_far, small, packed_weights
    )
    picks, gains, taps, skip, flags, row_first, places, which = small

    kept1, give1 = halve(which, [by_near, by_far])
    got1, kept1_far = across(give1), to_owner(kept1, far_owner)
    packed_weights, _ = tie(packed_weights, got1)
    weights = along_line(packed_weights)
    all0 = to_near([kept0, got0, kept0_far, got0_far])
    by_both, got1, kept1_far, all0 = tie(by_both, got1, kept1_far, all0)

    kept2, give2 = halve(which, [by_both])
    got2, kept2_far = across(give2), to_owner(kept2, far_owner)
    got1_far = to_owner(got1, far_owner)
    some1 = to_near([kept1, got1, kept1_far])
    normed0 = scaled([kept0, got0, kept0_far, got0_far, all0])
    got2, kept2_far, got1_far, some1, normed0 = tie(got2, kept2_far, got1_far, some1, normed0)

    got2_far = to_owner(got2, far_owner)
    rest1 = to_near([got1_far])
    near_kept2, near_kept2_far, near_got2 = [to_near([some]) for some in (kept2, kept2_far, got2)]
    got2_far, rest1, near_kept2, near_kept2_far, near_got2 = tie(
        got2_far, rest1, near_kept2, near_kept2_far, near_got2
    )

    near_got2_far = to_near([got2_far])
    normed1 = scaled([kept1, got1, kept1_far, got1_far, some1, rest1])
    normed2 = scaled([kept2, kept2_far, near_kept2, near_kept2_far])
    near_got2_far, normed1, normed2, weights = tie(near_got2_far, normed1, normed2, weights)

    near0, far0 = projected(0, [normed0])
    theirs0 = across(far0)
    near1, far1 = projected(0, [normed1, normed2])
    theirs1 = across(far1)
    normed3 = scaled([got2, got2_far, near_got2, near_got2_far])
    near3, far3 = projected(0, [normed3])
    theirs3 = across(far3)
    normed0, normed1, near3 = tie(normed0, normed1, near3)
    gate_near0, gate_far0 = projected(1, [normed0, normed1])
    gate_near3, gate_far3 = projected(1, [normed2, normed3], [row_count, 0])
    early = place(
        row_first, total_rows, near0, theirs0, places[:, :wide], tall, [kept0, got0]
    )
    early = place(
        row_first, total_rows, near1, theirs1, places[:, wide:-wide], tall, [kept1, got1], [early]
    )
    early, theirs3, gate_far0, gate_far3 = tie(early, theirs3, gate_far0, gate_far3)
    gate_theirs0, gate_theirs3 = across(gate_far0), across(gate_far3)
    banded, packed = band_of(
        flags, row_first, taps, skip, early, (near1, theirs1), (near3, theirs3),
        places[:, -wide:], tall, [kept2, got2],
    )
    early = place(row_first, total_rows, gate_near0, gate_theirs0, places[:, :-wide])
    mixed = mix(banded, packed, early, gate_near3, gate_theirs3, places[:, -wide:], shards)
    mixed = lax.all_to_all(mixed, "seq", split_axis=0, concat_axis=0, tiled=True)
    mixed = mixed.reshape(line, 2, width, row_count).transpose(1, 0, 2, 3)
    return mixed.reshape(features, row_count)


def solution(mesh):
    placed = (P("mp", "seq"), P(), P(), P("seq", "mp"), P("seq", "mp"), P("mp", None), P("mp"), P())
    shards, groups = mesh.shape["seq"], mesh.shape["mp"]

    def whole(*args):
        tokens, w_value, filters = args[0], args[3], args[5]
        moves_tokens = (
            tokens.shape[1] <= w_value.shape[1]
            and shards == 2 * groups
            and groups & (groups - 1) == 0
            and (groups - 1).bit_count() == 2
            and tokens.shape[0] % (LANES * shards * groups) == 0
            and filters.shape[1] % LANES == 0
            and tokens.shape[1] // shards % filters.shape[1] == 0
        )
        body = on_device_line if moves_tokens else on_device
        return jax.shard_map(
            body, mesh=mesh, in_specs=placed, out_specs=P("mp", "seq"), check_vma=False
        )(*args)

    return whole
```

```python
import functools
import math

import jax
import jax.numpy as jnp
from jax import lax
from jax.experimental import pallas as pl
from jax.experimental.pallas import tpu as pltpu
from jax.sharding import PartitionSpec as P

epsilon = 1e-05
AXES = ("seq", "mp")
LANES = 128
SUBLANES = 8
EXTRA = 2 * SUBLANES
VMEM = pl.BlockSpec(memory_space=pltpu.VMEM)
ANY = pl.BlockSpec(memory_space=pl.ANY)
SMEM = pl.BlockSpec(memory_space=pltpu.SMEM)
PARAMS = pltpu.CompilerParams(vmem_limit_bytes=16 * 1024 * 1024)


def toeplitz(filter_taps):
    chan_count, tap_count = filter_taps.shape
    padding = jnp.zeros((chan_count, tap_count), filter_taps.dtype)
    line_row = jnp.concatenate([padding, filter_taps[:, ::-1], padding], axis=1)
    tiled = jnp.tile(line_row, (1, tap_count))[:, : tap_count * (3 * tap_count - 1)]
    return tiled.reshape(chan_count, tap_count, 3 * tap_count - 1)[
        :, :, tap_count - 1 : 3 * tap_count - 1
    ]


def doc_flags(lengths, block_count, dtype):
    starts = jnp.cumsum(lengths, dtype=jnp.int32) - lengths
    block_index = jnp.arange(block_count, dtype=jnp.int32)
    is_start = jnp.any(block_index[:, None] == starts[None, :], axis=1)
    return jnp.where(is_start, 0.0, 1.0).astype(dtype)


def band_product(values, prior_rim, filter_taps, link_flags):
    chan_count, seq_length = values.shape
    tap_count = filter_taps.shape[1]
    block_count = seq_length // tap_count
    group_size = math.gcd(chan_count, 64)
    groups = chan_count // group_size

    def one_group(group_args):
        part_values, part_rim, part_taps = group_args
        blocks = part_values.reshape(group_size, block_count, tap_count)
        earlier = jnp.concatenate([part_rim[:, None, :], blocks[:, :-1, :]], axis=1)
        earlier = earlier * link_flags[None, :, None]
        joined = jnp.concatenate([earlier, blocks], axis=2)
        banded = jnp.einsum(
            "cpq,cbq->cbp", toeplitz(part_taps), joined, preferred_element_type=jnp.float32
        )
        return banded.reshape(group_size, seq_length)

    result = lax.map(
        one_group,
        (
            values.reshape(groups, group_size, seq_length),
            prior_rim.reshape(groups, group_size, tap_count),
            filter_taps.reshape(groups, group_size, tap_count),
        ),
    )
    return result.reshape(chan_count, seq_length)


def project_all(all_features, norm_gain, weight_pair):
    widened = all_features.astype(jnp.float32)
    inv_scale = lax.rsqrt(jnp.mean(widened * widened, axis=0, keepdims=True) + epsilon)
    normed = (widened * inv_scale * norm_gain[:, None]).astype(jnp.bfloat16)
    contract = (((0,), (0,)), ((), ()))
    value_part = lax.dot_general(
        weight_pair[0], normed, contract, preferred_element_type=jnp.float32
    ).astype(jnp.bfloat16)
    gate_part = lax.dot_general(
        weight_pair[1], normed, contract, preferred_element_type=jnp.float32
    ).astype(jnp.bfloat16)
    return (value_part, gate_part)


def on_device(tokens, packing, norm_gain, w_value, w_gate, filters, skip_gain, lengths):
    row_count = tokens.shape[1]
    shards = lax.axis_size("seq")
    my_index = lax.axis_index("seq")
    all_count = packing.shape[0]
    tap_count = filters.shape[1]
    chan_count = tokens.shape[0] // shards
    weight_pair = (
        lax.all_gather(w_value, "seq", axis=0, tiled=True),
        lax.all_gather(w_gate, "seq", axis=0, tiled=True),
    )
    inverse = (
        jnp.zeros((all_count,), jnp.int32).at[packing].set(jnp.arange(all_count, dtype=jnp.int32))
    )
    chan_taps = lax.dynamic_slice_in_dim(filters, my_index * chan_count, chan_count, 0)
    chan_skip = lax.dynamic_slice_in_dim(skip_gain, my_index * chan_count, chan_count, 0)
    slot_cap = 2 * (row_count // shards)
    own_packing = lax.dynamic_slice_in_dim(packing, my_index * row_count, row_count)
    dest_owner = own_packing // row_count
    onehot = (dest_owner[:, None] == jnp.arange(shards, dtype=jnp.int32)[None, :]).astype(jnp.int32)
    slot_rank = jnp.sum((jnp.cumsum(onehot, axis=0, dtype=jnp.int32) - onehot) * onehot, axis=1)
    slot_index = dest_owner * slot_cap + slot_rank
    send_buffer = (
        jnp.zeros((tokens.shape[0], shards * slot_cap), jnp.bfloat16).at[:, slot_index].set(tokens)
    )
    received = lax.all_to_all(send_buffer, "seq", split_axis=1, concat_axis=1, tiled=True)
    my_sources = lax.dynamic_slice_in_dim(inverse, my_index * row_count, row_count)
    to_me = (packing // row_count == my_index).astype(jnp.int32).reshape(shards, row_count)
    arrival_rank = (jnp.cumsum(to_me, axis=1, dtype=jnp.int32) - to_me).reshape(all_count)
    packed = received[:, my_sources // row_count * slot_cap + arrival_rank[my_sources]]
    all_features = lax.all_gather(packed, "mp", axis=0, tiled=True)
    value_part, gate_part = project_all(all_features, norm_gain, weight_pair)
    value_chan = lax.all_to_all(value_part, "seq", split_axis=0, concat_axis=1, tiled=True)
    link_flags = doc_flags(lengths, all_count // tap_count, jnp.bfloat16)
    prior_rim = jnp.zeros((chan_count, tap_count), jnp.bfloat16)
    banded = band_product(value_chan, prior_rim, chan_taps, link_flags)
    chan_band = (banded + chan_skip[:, None] * value_chan.astype(jnp.float32)).astype(jnp.bfloat16)
    mixed_band = lax.all_to_all(chan_band, "seq", split_axis=1, concat_axis=0, tiled=True)
    mixed_band = lax.optimization_barrier(mixed_band)
    gate_wide = lax.optimization_barrier(gate_part).astype(jnp.float32)
    return (packed.astype(jnp.float32) + gate_wide * mixed_band.astype(jnp.float32)).astype(
        jnp.bfloat16
    )


def halve_kernel(x_ref, token_ref, keep_ref, give_ref):
    features, count = token_ref.shape
    half = features // 2
    x = x_ref[0]
    widened = token_ref[...].astype(jnp.float32)
    rest = jnp.sum(widened * widened, axis=0, keepdims=True)
    terms = []
    for _ in range(3):
        term = rest.astype(jnp.bfloat16).astype(jnp.float32)
        terms.append(term)
        rest = rest - term
    row = lax.broadcasted_iota(jnp.int32, (EXTRA, count), 0)
    extra = jnp.zeros(row.shape, jnp.float32)
    for i, term in enumerate(terms):
        extra = jnp.where(row == i, term, extra)
    extra = extra.astype(jnp.bfloat16)
    for out_ref, which in ((keep_ref, x), (give_ref, 1 - x)):
        out_ref[0:half, :] = token_ref[pl.ds(pl.multiple_of(which * half, half), half), :]
        out_ref[half : half + EXTRA, :] = extra


def halve(x, tokens):
    features, count = tokens.shape
    out = jax.ShapeDtypeStruct((features // 2 + EXTRA, count), tokens.dtype)
    return pl.pallas_call(
        halve_kernel,
        out_shape=[out, out],
        in_specs=[SMEM, VMEM],
        out_specs=[VMEM, VMEM],
        compiler_params=PARAMS,
        cost_estimate=pl.CostEstimate(
            flops=2 * features * count, bytes_accessed=4 * features * count, transcendentals=0
        ),
    )(x, tokens)


def pack_kernel(after_ref, *refs):
    out_ref = refs[-1]
    line, _, _, width, _ = out_ref.shape
    for which, ref in enumerate(refs[:-1]):
        for target in range(line):
            for half in range(2):
                first = (half * line + target) * width
                out_ref[target, which, half] = ref[:, first : first + width].T


def pack_weights(after, weights, line):
    height, columns = weights[0].shape
    out = (line, len(weights), 2, columns // (2 * line), height)
    return pl.pallas_call(
        pack_kernel,
        out_shape=jax.ShapeDtypeStruct(out, weights[0].dtype),
        in_specs=[ANY] + [VMEM] * len(weights),
        out_specs=VMEM,
        compiler_params=PARAMS,
        cost_estimate=pl.CostEstimate(
            flops=0, bytes_accessed=4 * height * columns * len(weights), transcendentals=0
        ),
    )(after, *weights)


def scale_kernel(height, pick_ref, gain_ref, *refs):
    arrays, out_ref = refs[:-1], refs[-1]
    parts = out_ref.shape[0]
    tall = height + EXTRA
    blocks = [
        ref.at[first : first + tall] for ref in arrays for first in range(0, ref.shape[0], tall)
    ]
    each = len(blocks) // parts
    count = out_ref.shape[2] // each
    slots = each // 2 if each > 1 else 1
    features = 2 * height * parts
    gain_columns = gain_ref[...].T
    for number in range(each):
        slot, half = number % slots, number // slots
        first = (slot * (each // slots) + half) * count
        squares = jnp.zeros((1, count), jnp.float32)
        for block in blocks[number::each]:
            terms = block[height:tall, :].astype(jnp.float32)
            squares += jnp.sum(terms, axis=0, keepdims=True)
        inv_row = lax.rsqrt(squares / features + epsilon)
        for part in range(parts):
            scaled = blocks[part * each + number][0:height, :].astype(jnp.float32) * inv_row
            scaled = (scaled * gain_columns[:, part : part + 1]).astype(jnp.bfloat16)
            out_ref[pick_ref[part], :, first : first + count] = scaled


def scale(picks, gains, height, arrays):
    parts = picks.shape[0]
    count = arrays[0].shape[1]
    each = sum(array.shape[0] for array in arrays) // (height + EXTRA) // parts
    return pl.pallas_call(
        functools.partial(scale_kernel, height),
        out_shape=jax.ShapeDtypeStruct((parts, height, count * each), jnp.bfloat16),
        in_specs=[SMEM] + [VMEM] * (1 + len(arrays)),
        out_specs=VMEM,
        compiler_params=PARAMS,
        cost_estimate=pl.CostEstimate(
            flops=2 * parts * height * count * each,
            bytes_accessed=4 * parts * height * count * each,
            transcendentals=0,
        ),
    )(picks, gains, *arrays)


def project_kernel(number, row_count, x_ref, weight_ref, *refs):
    mine_ref, other_ref, mine, other = refs[-4:]
    x = x_ref[0]
    part = pl.program_id(0)

    @pl.when(part == 0)
    def _():
        mine[...] = jnp.zeros(mine.shape, jnp.float32)
        other[...] = jnp.zeros(mine.shape, jnp.float32)

    first = 0
    for ref in refs[:-4]:
        columns = slice(first, first + ref.shape[2])
        first = columns.stop
        block = ref[0]
        for which, total in ((x, mine), (1 - x, other)):
            total[:, columns] += jnp.dot(
                weight_ref[0, number, which], block, preferred_element_type=jnp.float32
            )

    @pl.when(part == pl.num_programs(0) - 1)
    def _():
        mine_ref[...] = mine[...]
        for begin in range(0, mine.shape[1], row_count):
            swapped = begin + row_count if begin // row_count % 2 == 0 else begin - row_count
            other_ref[:, begin : begin + row_count] = other[
                :, swapped : swapped + row_count
            ].astype(jnp.bfloat16)


def project(x, weights, number, normed, row_count):
    line, kinds, _, width, height = weights.shape
    out = (width, sum(some.shape[2] for some in normed))
    whole = pl.BlockSpec(out, lambda part: (0, 0))
    return pl.pallas_call(
        functools.partial(project_kernel, number, row_count),
        grid=(line,),
        out_shape=[
            jax.ShapeDtypeStruct(out, jnp.float32),
            jax.ShapeDtypeStruct(out, jnp.bfloat16),
        ],
        in_specs=[SMEM, pl.BlockSpec((1, kinds, 2, width, height), lambda part: (part, 0, 0, 0, 0))]
        + [pl.BlockSpec((1, *some.shape[1:]), lambda part: (part, 0, 0)) for some in normed],
        out_specs=[whole, whole],
        scratch_shapes=[pltpu.VMEM(out, jnp.float32)] * 2,
        compiler_params=PARAMS,
        cost_estimate=pl.CostEstimate(
            flops=4 * width * height * out[1] * line,
            bytes_accessed=weights.size + 2 * height * out[1] * line,
            transcendentals=0,
        ),
    )(x, weights, *normed)


def column_of(row):
    tall = jnp.broadcast_to(row.astype(jnp.float32), (SUBLANES, row.shape[1])).T
    return tall[:, 0:1].astype(row.dtype)


def at_places(array, place_row, total):
    spot = lax.broadcasted_iota(jnp.int32, (array.shape[1], total), 1)
    onehot = (column_of(place_row) == spot).astype(jnp.float32).astype(jnp.bfloat16)
    return jnp.dot(array, onehot, preferred_element_type=jnp.float32)


def with_tokens(first, tall, summed, token_refs):
    chan = summed.shape[0]
    first = pl.multiple_of(first, chan)
    tokens = []
    for kept_ref, got_ref in zip(token_refs[::2], token_refs[1::2]):
        for start in range(0, kept_ref.shape[0], tall):
            tokens += [ref[pl.ds(first + start, chan), :] for ref in (kept_ref, got_ref)]
    return jnp.concatenate([summed, jnp.concatenate(tokens, axis=1)], axis=0)


def place_kernel(tall, many, first_ref, mine_ref, theirs_ref, place_ref, *refs):
    tokens, before, out_ref = refs[:many], refs[many:-1], refs[-1]
    count = place_ref.shape[1]
    summed = mine_ref[:, :count] + theirs_ref[:, :count].astype(jnp.float32)
    summed = summed.astype(jnp.bfloat16)
    if tokens:
        summed = with_tokens(first_ref[0], tall, summed, tokens)
    moved = at_places(summed, place_ref[...], out_ref.shape[1])
    for ref in before:
        moved += ref[...].astype(jnp.float32)
    out_ref[...] = moved.astype(jnp.bfloat16)


def place(first, total, mine, theirs, places, tall=0, tokens=(), before=()):
    chan, count = mine.shape[0], places.shape[1]
    return pl.pallas_call(
        functools.partial(place_kernel, tall, len(tokens)),
        out_shape=jax.ShapeDtypeStruct((2 * chan if tokens else chan, total), jnp.bfloat16),
        in_specs=[SMEM] + [VMEM] * (3 + len(tokens) + len(before)),
        out_specs=VMEM,
        compiler_params=PARAMS,
        cost_estimate=pl.CostEstimate(
            flops=2 * chan * total * count, bytes_accessed=8 * chan * total, transcendentals=0
        ),
    )(first, mine, theirs, places, *tokens, *before)


def band_kernel(
    taps_blocks, tall, flag_ref, first_ref, taps_ref, skip_ref, early_ref, mine_ref, theirs_ref,
    place_ref, *refs
):
    shifted = refs[-taps_blocks - 1 :]
    out_ref, packed_ref, whole, band = refs[-taps_blocks - 5 : -taps_blocks - 1]
    chan = taps_ref.shape[0]
    total = whole.shape[1]
    pieces = total // LANES
    summed = (mine_ref[...] + theirs_ref[...].astype(jnp.float32)).astype(jnp.bfloat16)
    summed = with_tokens(first_ref[0], tall, summed, refs[: -taps_blocks - 5])
    moved = at_places(summed, place_ref[...], total) + early_ref[...].astype(jnp.float32)
    whole[...] = moved[0:chan]
    packed_ref[...] = moved[chan : 2 * chan].astype(jnp.bfloat16)
    for piece in range(pieces):
        for back in range(taps_blocks + 1):
            rows = pl.ds(piece * chan, chan)
            if back > piece:
                shifted[back][rows, :] = jnp.zeros((chan, LANES), jnp.float32)
                continue
            first = (piece - back) * LANES
            part = whole[:, first : first + LANES]
            if back > piece % taps_blocks:
                part = part * flag_ref[piece // taps_blocks]
            shifted[back][rows, :] = part
    column = lax.broadcasted_iota(jnp.int32, (LANES, LANES), 1)
    row = lax.broadcasted_iota(jnp.int32, (LANES, LANES), 0)
    later = column >= row
    zero = jnp.zeros((LANES, LANES), jnp.float32)

    def one(group, carry):
        base = pl.multiple_of(group * SUBLANES, SUBLANES)
        group_taps = taps_ref[pl.ds(base, SUBLANES), :]
        for member in range(SUBLANES):
            turned = [zero]
            for block in range(taps_blocks):
                line_row = group_taps[member : member + 1, block * LANES : (block + 1) * LANES]
                square = jnp.broadcast_to(line_row, (LANES, LANES))
                turned.append(pltpu.roll(square, 0, 1, stride=1, stride_axis=0))
            turned.append(zero)
            rows = pl.ds(base + member, pieces, stride=chan)
            tiles, inputs = [], []
            for back in range(taps_blocks + 1):
                tiles.append(jnp.where(later, turned[back + 1], turned[back]).astype(jnp.bfloat16))
                inputs.append(shifted[back][rows, :].astype(jnp.bfloat16))
            band[rows, :] = jnp.dot(
                jnp.concatenate(inputs, axis=1),
                jnp.concatenate(tiles, axis=0),
                preferred_element_type=jnp.float32,
            )
        return carry

    lax.fori_loop(0, chan // SUBLANES, one, 0)
    skip = column_of(skip_ref[...])
    for piece in range(pieces):
        lanes = slice(piece * LANES, (piece + 1) * LANES)
        rows = pl.ds(piece * chan, chan)
        out_ref[:, lanes] = (band[rows, :] + skip * whole[:, lanes]).astype(jnp.bfloat16)


def band_of(flags, first, taps, skip, early, mine, theirs, places, tall, tokens):
    chan, tap_count = taps.shape
    total = early.shape[1]
    taps_blocks = tap_count // LANES
    tower = (total // LANES * chan, LANES)
    out = jax.ShapeDtypeStruct((chan, total), jnp.bfloat16)
    return pl.pallas_call(
        functools.partial(band_kernel, taps_blocks, tall),
        out_shape=[out, out],
        in_specs=[SMEM, SMEM] + [VMEM] * (6 + len(tokens)),
        out_specs=[VMEM, VMEM],
        scratch_shapes=[pltpu.VMEM((chan, total), jnp.float32)]
        + [pltpu.VMEM(tower, jnp.float32)] * (taps_blocks + 2),
        compiler_params=PARAMS,
        cost_estimate=pl.CostEstimate(
            flops=3 * chan * total * total, bytes_accessed=16 * chan * total, transcendentals=0
        ),
    )(flags, first, taps, skip, early, mine, theirs, places, *tokens)


def mix_kernel(z_ref, packed_ref, early_ref, mine_ref, theirs_ref, place_ref, out_ref):
    summed = (mine_ref[...] + theirs_ref[...].astype(jnp.float32)).astype(jnp.bfloat16)
    gate = at_places(summed, place_ref[...], z_ref.shape[1]) + early_ref[...].astype(jnp.float32)
    mixed = packed_ref[...].astype(jnp.float32) + gate * z_ref[...].astype(jnp.float32)
    mixed = mixed.astype(jnp.bfloat16)
    wide = out_ref.shape[2]
    pairs = out_ref.shape[0] // 2
    for place in range(2 * pairs):
        owner = place % pairs * 2 + place // pairs
        out_ref[place] = mixed[:, owner * wide : (owner + 1) * wide]


def mix(z, packed, early, mine, theirs, places, shards):
    chan, total = z.shape
    return pl.pallas_call(
        mix_kernel,
        out_shape=jax.ShapeDtypeStruct((shards, chan, total // shards), jnp.bfloat16),
        in_specs=[VMEM] * 6,
        out_specs=VMEM,
        compiler_params=PARAMS,
        cost_estimate=pl.CostEstimate(
            flops=chan * total * total, bytes_accessed=16 * chan * total, transcendentals=0
        ),
    )(z, packed, early, mine, theirs, places)


def on_device_line(tokens, packing, norm_gain, w_value, w_gate, filters, skip_gain, lengths):
    shards, groups = lax.axis_size("seq"), lax.axis_size("mp")
    line = shards // 2
    s, m = lax.axis_index("seq"), lax.axis_index("mp")
    z, x = s // 2, s % 2
    features, row_count = tokens.shape
    half = features // 2
    total_rows = packing.shape[0]
    width = features // shards

    def number(zz, xx, mm):
        return (zz * 2 + xx) * groups + mm

    def send(array, target):
        pairs = []
        for zz in range(line):
            for xx in range(2):
                for mm in range(groups):
                    to = target(zz, xx, mm)
                    if to is not None:
                        pairs.append((number(zz, xx, mm), number(*to)))
        return lax.ppermute(array, AXES, pairs)

    def across(array):
        return send(array, lambda zz, xx, mm: (zz, 1 - xx, mm))

    def to_owner(array, o):
        return send(array, lambda zz, xx, mm: (zz, xx, mm ^ o))

    columns = [[number(zz, xx, mm) for zz in range(line)] for xx in range(2) for mm in range(groups)]

    def along_line(array):
        return lax.all_to_all(
            array, AXES, split_axis=0, concat_axis=0, tiled=True, axis_index_groups=columns
        )

    def to_pair(array, o):
        return send(array, lambda zz, xx, mm: (zz ^ o, xx, mm))

    slot_pair = jnp.stack([z ^ o for o in range(line)])
    far_owner, near_owner, far_pair, near_pair = groups // 2, groups // 4, line // 2, line // 4
    owners = jnp.stack([m ^ o for o in (0, far_owner, near_owner, far_owner ^ near_owner)])
    which = x[None].astype(jnp.int32)
    picks = owners.astype(jnp.int32)
    gains = norm_gain.reshape(groups, 2, half)[:, x][owners]
    gains = jnp.pad(gains, ((0, -groups % SUBLANES), (0, 0)))
    places = packing.reshape(line, 2, row_count)[slot_pair]
    places = jnp.stack([places[:, x], places[:, 1 - x]], axis=1).reshape(1, total_rows)
    first = x * half + z * width
    taps = lax.dynamic_slice_in_dim(filters, first, width, 0).astype(jnp.float32)
    skip = lax.dynamic_slice_in_dim(skip_gain, first, width, 0)[None]
    flags = doc_flags(lengths, total_rows // filters.shape[1], jnp.float32)
    row_first = (z * width)[None].astype(jnp.int32)
    tall = half + EXTRA
    wide = 2 * row_count

    def projected(number, some):
        return project(which, weights, number, some, row_count)

    def scaled(arrays):
        return scale(picks, gains, half, arrays)

    def to_near(arrays):
        stacked = jnp.concatenate(arrays, axis=0) if len(arrays) > 1 else arrays[0]
        return to_owner(stacked, near_owner)

    def tie(*arrays):
        return lax.optimization_barrier(arrays)

    by_far, by_near = to_pair(tokens, far_pair), to_pair(tokens, near_pair)
    kept0, give0 = halve(which, tokens)
    got0, kept0_far = across(give0), to_owner(kept0, far_owner)
    got0_far = to_owner(got0, far_owner)
    packed_weights = pack_weights(give0, [w_value, w_gate], line)
    packed_weights, by_near = tie(packed_weights, by_near)
    kept1, give1 = halve(which, by_near)
    small = picks, gains, taps, skip, flags, row_first, places, which
    by_both = to_pair(by_far, near_pair)
    by_far, got0, kept0_far, got0_far, kept1, give1, small, packed_weights = tie(
        by_far, got0, kept0_far, got0_far, kept1, give1, small, packed_weights
    )
    picks, gains, taps, skip, flags, row_first, places, which = small

    kept2, give2 = halve(which, by_far)
    got1, kept1_far = across(give1), to_owner(kept1, far_owner)
    got2, kept2_far = across(give2), to_owner(kept2, far_owner)
    got1_far = to_owner(got1, far_owner)
    weights = along_line(packed_weights)
    all0 = to_near([kept0, got0, kept0_far, got0_far])
    by_both, got1, kept1_far, got1_far, got2, kept2_far, all0 = tie(
        by_both, got1, kept1_far, got1_far, got2, kept2_far, all0
    )

    kept3, give3 = halve(which, by_both)
    got3, kept3_far = across(give3), to_owner(kept3, far_owner)
    got2_far = to_owner(got2, far_owner)
    all1 = to_near([kept1, got1, kept1_far, got1_far])
    normed0 = scaled([kept0, got0, kept0_far, got0_far, all0])
    got3, kept3_far, got2_far, all1, normed0 = tie(got3, kept3_far, got2_far, all1, normed0)

    got3_far = to_owner(got3, far_owner)
    all2 = to_near([kept2, got2, kept2_far, got2_far])
    near_kept3, near_kept3_far, near_got3 = [to_near([some]) for some in (kept3, kept3_far, got3)]
    normed1 = scaled([kept1, got1, kept1_far, got1_far, all1])
    got3_far, all2, near_kept3, near_kept3_far, near_got3, normed1 = tie(
        got3_far, all2, near_kept3, near_kept3_far, near_got3, normed1
    )

    near_got3_far = to_near([got3_far])
    normed2 = scaled([kept2, got2, kept2_far, got2_far, all2])
    near_got3_far, normed2 = tie(near_got3_far, normed2)
    normed3 = scaled(
        [kept3, got3, kept3_far, got3_far, near_kept3, near_got3, near_kept3_far, near_got3_far]
    )
    normed3, weights = tie(normed3, weights)

    cut = 2 * wide
    value0, far0 = projected(0, [normed0, normed1])
    theirs0 = across(far0)
    value0, normed2 = tie(value0, normed2)
    value2, far2 = projected(0, [normed2, normed3])
    theirs2 = across(far2)
    normed0, value2 = tie(normed0, value2)
    gate0, gate_far0 = projected(1, [normed0, normed1])
    gate2, gate_far2 = projected(1, [normed2, normed3])
    early = place(
        row_first, total_rows, value0, theirs0, places[:, :cut], tall, [kept0, got0, kept1, got1]
    )
    early, theirs2, gate_far0, gate_far2 = tie(early, theirs2, gate_far0, gate_far2)
    gate_theirs0, gate_theirs2 = across(gate_far0), across(gate_far2)
    banded, packed = band_of(
        flags, row_first, taps, skip, early, value2, theirs2, places[:, cut:], tall,
        [kept2, got2, kept3, got3],
    )
    early = place(row_first, total_rows, gate0, gate_theirs0, places[:, :cut])
    mixed = mix(banded, packed, early, gate2, gate_theirs2, places[:, cut:], shards)
    owners = [[number(zz, xx, mm) for xx in range(2) for zz in range(line)] for mm in range(groups)]
    mixed = lax.all_to_all(
        mixed, AXES, split_axis=0, concat_axis=0, tiled=True, axis_index_groups=owners
    )
    return mixed.reshape(features, row_count)


def solution(mesh):
    placed = (P("mp", "seq"), P(), P(), P("seq", "mp"), P("seq", "mp"), P("mp", None), P("mp"), P())
    shards, groups = mesh.shape["seq"], mesh.shape["mp"]

    def whole(*args):
        tokens, w_value, filters = args[0], args[3], args[5]
        moves_tokens = (
            tokens.shape[1] <= w_value.shape[1]
            and shards == 2 * groups
            and groups & (groups - 1) == 0
            and (groups - 1).bit_count() == 2
            and tokens.shape[0] % (LANES * shards * groups) == 0
            and filters.shape[1] % LANES == 0
            and tokens.shape[1] // shards % filters.shape[1] == 0
        )
        body = on_device_line if moves_tokens else on_device
        return jax.shard_map(
            body, mesh=mesh, in_specs=placed, out_specs=P("mp", "seq"), check_vma=False
        )(*args)

    return whole
```

```python
import functools
import math

import jax
import jax.numpy as jnp
from jax import lax
from jax.experimental import pallas as pl
from jax.experimental.pallas import tpu as pltpu
from jax.sharding import PartitionSpec as P

epsilon = 1e-05
AXES = ("seq", "mp")
LANES = 128
SUBLANES = 8
EXTRA = 2 * SUBLANES
VMEM = pl.BlockSpec(memory_space=pltpu.VMEM)
ANY = pl.BlockSpec(memory_space=pl.ANY)
SMEM = pl.BlockSpec(memory_space=pltpu.SMEM)
PARAMS = pltpu.CompilerParams(vmem_limit_bytes=16 * 1024 * 1024)


def toeplitz(filter_taps):
    chan_count, tap_count = filter_taps.shape
    padding = jnp.zeros((chan_count, tap_count), filter_taps.dtype)
    line_row = jnp.concatenate([padding, filter_taps[:, ::-1], padding], axis=1)
    tiled = jnp.tile(line_row, (1, tap_count))[:, : tap_count * (3 * tap_count - 1)]
    return tiled.reshape(chan_count, tap_count, 3 * tap_count - 1)[
        :, :, tap_count - 1 : 3 * tap_count - 1
    ]


def doc_flags(lengths, block_count, dtype):
    starts = jnp.cumsum(lengths, dtype=jnp.int32) - lengths
    block_index = jnp.arange(block_count, dtype=jnp.int32)
    is_start = jnp.any(block_index[:, None] == starts[None, :], axis=1)
    return jnp.where(is_start, 0.0, 1.0).astype(dtype)


def band_product(values, prior_rim, filter_taps, link_flags):
    chan_count, seq_length = values.shape
    tap_count = filter_taps.shape[1]
    block_count = seq_length // tap_count
    group_size = math.gcd(chan_count, 64)
    groups = chan_count // group_size

    def one_group(group_args):
        part_values, part_rim, part_taps = group_args
        blocks = part_values.reshape(group_size, block_count, tap_count)
        earlier = jnp.concatenate([part_rim[:, None, :], blocks[:, :-1, :]], axis=1)
        earlier = earlier * link_flags[None, :, None]
        joined = jnp.concatenate([earlier, blocks], axis=2)
        banded = jnp.einsum(
            "cpq,cbq->cbp", toeplitz(part_taps), joined, preferred_element_type=jnp.float32
        )
        return banded.reshape(group_size, seq_length)

    result = lax.map(
        one_group,
        (
            values.reshape(groups, group_size, seq_length),
            prior_rim.reshape(groups, group_size, tap_count),
            filter_taps.reshape(groups, group_size, tap_count),
        ),
    )
    return result.reshape(chan_count, seq_length)


def project_all(all_features, norm_gain, weight_pair):
    widened = all_features.astype(jnp.float32)
    inv_scale = lax.rsqrt(jnp.mean(widened * widened, axis=0, keepdims=True) + epsilon)
    normed = (widened * inv_scale * norm_gain[:, None]).astype(jnp.bfloat16)
    contract = (((0,), (0,)), ((), ()))
    value_part = lax.dot_general(
        weight_pair[0], normed, contract, preferred_element_type=jnp.float32
    ).astype(jnp.bfloat16)
    gate_part = lax.dot_general(
        weight_pair[1], normed, contract, preferred_element_type=jnp.float32
    ).astype(jnp.bfloat16)
    return (value_part, gate_part)


def on_device(tokens, packing, norm_gain, w_value, w_gate, filters, skip_gain, lengths):
    row_count = tokens.shape[1]
    shards = lax.axis_size("seq")
    my_index = lax.axis_index("seq")
    all_count = packing.shape[0]
    tap_count = filters.shape[1]
    chan_count = tokens.shape[0] // shards
    weight_pair = (
        lax.all_gather(w_value, "seq", axis=0, tiled=True),
        lax.all_gather(w_gate, "seq", axis=0, tiled=True),
    )
    inverse = (
        jnp.zeros((all_count,), jnp.int32).at[packing].set(jnp.arange(all_count, dtype=jnp.int32))
    )
    chan_taps = lax.dynamic_slice_in_dim(filters, my_index * chan_count, chan_count, 0)
    chan_skip = lax.dynamic_slice_in_dim(skip_gain, my_index * chan_count, chan_count, 0)
    slot_cap = 2 * (row_count // shards)
    own_packing = lax.dynamic_slice_in_dim(packing, my_index * row_count, row_count)
    dest_owner = own_packing // row_count
    onehot = (dest_owner[:, None] == jnp.arange(shards, dtype=jnp.int32)[None, :]).astype(jnp.int32)
    slot_rank = jnp.sum((jnp.cumsum(onehot, axis=0, dtype=jnp.int32) - onehot) * onehot, axis=1)
    slot_index = dest_owner * slot_cap + slot_rank
    send_buffer = (
        jnp.zeros((tokens.shape[0], shards * slot_cap), jnp.bfloat16).at[:, slot_index].set(tokens)
    )
    received = lax.all_to_all(send_buffer, "seq", split_axis=1, concat_axis=1, tiled=True)
    my_sources = lax.dynamic_slice_in_dim(inverse, my_index * row_count, row_count)
    to_me = (packing // row_count == my_index).astype(jnp.int32).reshape(shards, row_count)
    arrival_rank = (jnp.cumsum(to_me, axis=1, dtype=jnp.int32) - to_me).reshape(all_count)
    packed = received[:, my_sources // row_count * slot_cap + arrival_rank[my_sources]]
    all_features = lax.all_gather(packed, "mp", axis=0, tiled=True)
    value_part, gate_part = project_all(all_features, norm_gain, weight_pair)
    value_chan = lax.all_to_all(value_part, "seq", split_axis=0, concat_axis=1, tiled=True)
    link_flags = doc_flags(lengths, all_count // tap_count, jnp.bfloat16)
    prior_rim = jnp.zeros((chan_count, tap_count), jnp.bfloat16)
    banded = band_product(value_chan, prior_rim, chan_taps, link_flags)
    chan_band = (banded + chan_skip[:, None] * value_chan.astype(jnp.float32)).astype(jnp.bfloat16)
    mixed_band = lax.all_to_all(chan_band, "seq", split_axis=1, concat_axis=0, tiled=True)
    mixed_band = lax.optimization_barrier(mixed_band)
    gate_wide = lax.optimization_barrier(gate_part).astype(jnp.float32)
    return (packed.astype(jnp.float32) + gate_wide * mixed_band.astype(jnp.float32)).astype(
        jnp.bfloat16
    )


def halve_kernel(x_ref, token_ref, keep_ref, give_ref):
    features, count = token_ref.shape
    half = features // 2
    x = x_ref[0]
    widened = token_ref[...].astype(jnp.float32)
    rest = jnp.sum(widened * widened, axis=0, keepdims=True)
    terms = []
    for _ in range(3):
        term = rest.astype(jnp.bfloat16).astype(jnp.float32)
        terms.append(term)
        rest = rest - term
    row = lax.broadcasted_iota(jnp.int32, (EXTRA, count), 0)
    extra = jnp.zeros(row.shape, jnp.float32)
    for i, term in enumerate(terms):
        extra = jnp.where(row == i, term, extra)
    extra = extra.astype(jnp.bfloat16)
    for out_ref, which in ((keep_ref, x), (give_ref, 1 - x)):
        out_ref[0:half, :] = token_ref[pl.ds(pl.multiple_of(which * half, half), half), :]
        out_ref[half : half + EXTRA, :] = extra


def halve(x, tokens):
    features, count = tokens.shape
    out = jax.ShapeDtypeStruct((features // 2 + EXTRA, count), tokens.dtype)
    return pl.pallas_call(
        halve_kernel,
        out_shape=[out, out],
        in_specs=[SMEM, VMEM],
        out_specs=[VMEM, VMEM],
        compiler_params=PARAMS,
        cost_estimate=pl.CostEstimate(
            flops=2 * features * count, bytes_accessed=4 * features * count, transcendentals=0
        ),
    )(x, tokens)


def pack_kernel(after_ref, *refs):
    out_ref = refs[-1]
    line, _, _, width, _ = out_ref.shape
    for which, ref in enumerate(refs[:-1]):
        for target in range(line):
            for half in range(2):
                first = (half * line + target) * width
                out_ref[target, which, half] = ref[:, first : first + width].T


def pack_weights(after, weights, line):
    height, columns = weights[0].shape
    out = (line, len(weights), 2, columns // (2 * line), height)
    return pl.pallas_call(
        pack_kernel,
        out_shape=jax.ShapeDtypeStruct(out, weights[0].dtype),
        in_specs=[ANY] + [VMEM] * len(weights),
        out_specs=VMEM,
        compiler_params=PARAMS,
        cost_estimate=pl.CostEstimate(
            flops=0, bytes_accessed=4 * height * columns * len(weights), transcendentals=0
        ),
    )(after, *weights)


def scale_kernel(height, pick_ref, gain_ref, *refs):
    arrays, out_ref = refs[:-1], refs[-1]
    parts = out_ref.shape[0]
    tall = height + EXTRA
    blocks = [
        ref.at[first : first + tall] for ref in arrays for first in range(0, ref.shape[0], tall)
    ]
    each = len(blocks) // parts
    count = out_ref.shape[2] // each
    slots = each // 2 if each > 1 else 1
    features = 2 * height * parts
    gain_columns = gain_ref[...].T
    for number in range(each):
        slot, half = number % slots, number // slots
        first = (slot * (each // slots) + half) * count
        squares = jnp.zeros((1, count), jnp.float32)
        for block in blocks[number::each]:
            terms = block[height:tall, :].astype(jnp.float32)
            squares += jnp.sum(terms, axis=0, keepdims=True)
        inv_row = lax.rsqrt(squares / features + epsilon)
        for part in range(parts):
            scaled = blocks[part * each + number][0:height, :].astype(jnp.float32) * inv_row
            scaled = (scaled * gain_columns[:, part : part + 1]).astype(jnp.bfloat16)
            out_ref[pick_ref[part], :, first : first + count] = scaled


def scale(picks, gains, height, arrays):
    parts = picks.shape[0]
    count = arrays[0].shape[1]
    each = sum(array.shape[0] for array in arrays) // (height + EXTRA) // parts
    return pl.pallas_call(
        functools.partial(scale_kernel, height),
        out_shape=jax.ShapeDtypeStruct((parts, height, count * each), jnp.bfloat16),
        in_specs=[SMEM] + [VMEM] * (1 + len(arrays)),
        out_specs=VMEM,
        compiler_params=PARAMS,
        cost_estimate=pl.CostEstimate(
            flops=2 * parts * height * count * each,
            bytes_accessed=4 * parts * height * count * each,
            transcendentals=0,
        ),
    )(picks, gains, *arrays)


def project_kernel(number, row_count, x_ref, weight_ref, *refs):
    mine_ref, other_ref = refs[-2:]
    x = x_ref[0]
    first = 0
    for ref in refs[:-2]:
        parts, _, count = ref.shape
        mine = jnp.zeros((mine_ref.shape[0], count), jnp.float32)
        other = jnp.zeros((mine_ref.shape[0], count), jnp.float32)
        for part in range(parts):
            block = ref[part]
            mine += jnp.dot(
                weight_ref[part, number, x], block, preferred_element_type=jnp.float32
            )
            other += jnp.dot(
                weight_ref[part, number, 1 - x], block, preferred_element_type=jnp.float32
            )
        mine_ref[:, first : first + count] = mine
        other = other.astype(jnp.bfloat16)
        other_ref[:, first : first + row_count] = other[:, row_count:]
        other_ref[:, first + row_count : first + count] = other[:, :row_count]
        first += count


def project(x, weights, number, normed, row_count):
    line, _, _, width, height = weights.shape
    out = (width, sum(some.shape[2] for some in normed))
    return pl.pallas_call(
        functools.partial(project_kernel, number, row_count),
        out_shape=[
            jax.ShapeDtypeStruct(out, jnp.float32),
            jax.ShapeDtypeStruct(out, jnp.bfloat16),
        ],
        in_specs=[SMEM] + [VMEM] * (1 + len(normed)),
        out_specs=[VMEM, VMEM],
        compiler_params=PARAMS,
        cost_estimate=pl.CostEstimate(
            flops=4 * width * height * out[1] * line,
            bytes_accessed=weights.size + 2 * height * out[1] * line,
            transcendentals=0,
        ),
    )(x, weights, *normed)


def column_of(row):
    tall = jnp.broadcast_to(row.astype(jnp.float32), (SUBLANES, row.shape[1])).T
    return tall[:, 0:1].astype(row.dtype)


def at_places(array, place_row, total):
    spot = lax.broadcasted_iota(jnp.int32, (array.shape[1], total), 1)
    onehot = (column_of(place_row) == spot).astype(jnp.float32).astype(jnp.bfloat16)
    return jnp.dot(array, onehot, preferred_element_type=jnp.float32)


def with_tokens(first, tall, summed, token_refs):
    chan = summed.shape[0]
    first = pl.multiple_of(first, chan)
    tokens = []
    for kept_ref, got_ref in zip(token_refs[::2], token_refs[1::2]):
        for start in range(0, kept_ref.shape[0], tall):
            tokens += [ref[pl.ds(first + start, chan), :] for ref in (kept_ref, got_ref)]
    return jnp.concatenate([summed, jnp.concatenate(tokens, axis=1)], axis=0)


def place_kernel(tall, many, first_ref, mine_ref, theirs_ref, place_ref, *refs):
    tokens, before, out_ref = refs[:many], refs[many:-1], refs[-1]
    count = place_ref.shape[1]
    summed = mine_ref[:, :count] + theirs_ref[:, :count].astype(jnp.float32)
    summed = summed.astype(jnp.bfloat16)
    if tokens:
        summed = with_tokens(first_ref[0], tall, summed, tokens)
    moved = at_places(summed, place_ref[...], out_ref.shape[1])
    for ref in before:
        moved += ref[...].astype(jnp.float32)
    out_ref[...] = moved.astype(jnp.bfloat16)


def place(first, total, mine, theirs, places, tall=0, tokens=(), before=()):
    chan, count = mine.shape[0], places.shape[1]
    return pl.pallas_call(
        functools.partial(place_kernel, tall, len(tokens)),
        out_shape=jax.ShapeDtypeStruct((2 * chan if tokens else chan, total), jnp.bfloat16),
        in_specs=[SMEM] + [VMEM] * (3 + len(tokens) + len(before)),
        out_specs=VMEM,
        compiler_params=PARAMS,
        cost_estimate=pl.CostEstimate(
            flops=2 * chan * total * count, bytes_accessed=8 * chan * total, transcendentals=0
        ),
    )(first, mine, theirs, places, *tokens, *before)


def band_kernel(
    taps_blocks, tall, flag_ref, first_ref, taps_ref, skip_ref, early_ref, mine_ref, theirs_ref,
    place_ref, *refs
):
    shifted = refs[-taps_blocks - 1 :]
    out_ref, packed_ref, whole, band = refs[-taps_blocks - 5 : -taps_blocks - 1]
    chan = taps_ref.shape[0]
    total = whole.shape[1]
    pieces = total // LANES
    summed = (mine_ref[...] + theirs_ref[...].astype(jnp.float32)).astype(jnp.bfloat16)
    summed = with_tokens(first_ref[0], tall, summed, refs[: -taps_blocks - 5])
    moved = at_places(summed, place_ref[...], total) + early_ref[...].astype(jnp.float32)
    whole[...] = moved[0:chan]
    packed_ref[...] = moved[chan : 2 * chan].astype(jnp.bfloat16)
    for piece in range(pieces):
        for back in range(taps_blocks + 1):
            rows = pl.ds(piece * chan, chan)
            if back > piece:
                shifted[back][rows, :] = jnp.zeros((chan, LANES), jnp.float32)
                continue
            first = (piece - back) * LANES
            part = whole[:, first : first + LANES]
            if back > piece % taps_blocks:
                part = part * flag_ref[piece // taps_blocks]
            shifted[back][rows, :] = part
    column = lax.broadcasted_iota(jnp.int32, (LANES, LANES), 1).astype(jnp.bfloat16)
    row = lax.broadcasted_iota(jnp.int32, (LANES, LANES), 0).astype(jnp.bfloat16)
    later = column >= row
    zero = jnp.zeros((LANES, LANES), jnp.bfloat16)

    def one(group, carry):
        base = pl.multiple_of(group * SUBLANES, SUBLANES)
        group_taps = taps_ref[pl.ds(base, SUBLANES), :]
        for member in range(SUBLANES):
            turned = [zero]
            for block in range(taps_blocks):
                line_row = group_taps[member : member + 1, block * LANES : (block + 1) * LANES]
                square = jnp.broadcast_to(line_row, (LANES, LANES))
                square = pltpu.roll(square, 0, 1, stride=1, stride_axis=0)
                turned.append(square.astype(jnp.bfloat16))
            turned.append(zero)
            rows = pl.ds(base + member, pieces, stride=chan)
            tiles, inputs = [], []
            for back in range(taps_blocks + 1):
                tiles.append(jnp.where(later, turned[back + 1], turned[back]))
                inputs.append(shifted[back][rows, :].astype(jnp.bfloat16))
            band[rows, :] = jnp.dot(
                jnp.concatenate(inputs, axis=1),
                jnp.concatenate(tiles, axis=0),
                preferred_element_type=jnp.float32,
            )
        return carry

    lax.fori_loop(0, chan // SUBLANES, one, 0, unroll=4)
    skip = column_of(skip_ref[...])
    for piece in range(pieces):
        lanes = slice(piece * LANES, (piece + 1) * LANES)
        rows = pl.ds(piece * chan, chan)
        out_ref[:, lanes] = (band[rows, :] + skip * whole[:, lanes]).astype(jnp.bfloat16)


def band_of(flags, first, taps, skip, early, mine, theirs, places, tall, tokens):
    chan, tap_count = taps.shape
    total = early.shape[1]
    taps_blocks = tap_count // LANES
    tower = (total // LANES * chan, LANES)
    out = jax.ShapeDtypeStruct((chan, total), jnp.bfloat16)
    return pl.pallas_call(
        functools.partial(band_kernel, taps_blocks, tall),
        out_shape=[out, out],
        in_specs=[SMEM, SMEM] + [VMEM] * (6 + len(tokens)),
        out_specs=[VMEM, VMEM],
        scratch_shapes=[pltpu.VMEM((chan, total), jnp.float32)]
        + [pltpu.VMEM(tower, jnp.float32)] * (taps_blocks + 2),
        compiler_params=PARAMS,
        cost_estimate=pl.CostEstimate(
            flops=3 * chan * total * total, bytes_accessed=16 * chan * total, transcendentals=0
        ),
    )(flags, first, taps, skip, early, mine, theirs, places, *tokens)


def mix_kernel(z_ref, packed_ref, early_ref, mine_ref, theirs_ref, place_ref, out_ref):
    summed = (mine_ref[...] + theirs_ref[...].astype(jnp.float32)).astype(jnp.bfloat16)
    gate = at_places(summed, place_ref[...], z_ref.shape[1]) + early_ref[...].astype(jnp.float32)
    mixed = packed_ref[...].astype(jnp.float32) + gate * z_ref[...].astype(jnp.float32)
    mixed = mixed.astype(jnp.bfloat16)
    wide = out_ref.shape[2]
    pairs = out_ref.shape[0] // 2
    for place in range(2 * pairs):
        owner = place % pairs * 2 + place // pairs
        out_ref[place] = mixed[:, owner * wide : (owner + 1) * wide]


def mix(z, packed, early, mine, theirs, places, shards):
    chan, total = z.shape
    return pl.pallas_call(
        mix_kernel,
        out_shape=jax.ShapeDtypeStruct((shards, chan, total // shards), jnp.bfloat16),
        in_specs=[VMEM] * 6,
        out_specs=VMEM,
        compiler_params=PARAMS,
        cost_estimate=pl.CostEstimate(
            flops=chan * total * total, bytes_accessed=16 * chan * total, transcendentals=0
        ),
    )(z, packed, early, mine, theirs, places)


def on_device_line(tokens, packing, norm_gain, w_value, w_gate, filters, skip_gain, lengths):
    shards, groups = lax.axis_size("seq"), lax.axis_size("mp")
    line = shards // 2
    s, m = lax.axis_index("seq"), lax.axis_index("mp")
    z, x = s // 2, s % 2
    features, row_count = tokens.shape
    half = features // 2
    total_rows = packing.shape[0]
    width = features // shards

    def number(zz, xx, mm):
        return (zz * 2 + xx) * groups + mm

    def send(array, target):
        pairs = []
        for zz in range(line):
            for xx in range(2):
                for mm in range(groups):
                    to = target(zz, xx, mm)
                    if to is not None:
                        pairs.append((number(zz, xx, mm), number(*to)))
        return lax.ppermute(array, AXES, pairs)

    def across(array):
        return send(array, lambda zz, xx, mm: (zz, 1 - xx, mm))

    def to_owner(array, o):
        return send(array, lambda zz, xx, mm: (zz, xx, mm ^ o))

    columns = [[number(zz, xx, mm) for zz in range(line)] for xx in range(2) for mm in range(groups)]

    def along_line(array):
        return lax.all_to_all(
            array, AXES, split_axis=0, concat_axis=0, tiled=True, axis_index_groups=columns
        )

    def to_pair(array, o):
        return send(array, lambda zz, xx, mm: (zz ^ o, xx, mm))

    slot_pair = jnp.stack([z ^ o for o in range(line)])
    far_owner, near_owner, far_pair, near_pair = groups // 2, groups // 4, line // 2, line // 4
    owners = jnp.stack([m ^ o for o in (0, far_owner, near_owner, far_owner ^ near_owner)])
    which = x[None].astype(jnp.int32)
    picks = owners.astype(jnp.int32)
    gains = norm_gain.reshape(groups, 2, half)[:, x][owners]
    gains = jnp.pad(gains, ((0, -groups % SUBLANES), (0, 0)))
    places = packing.reshape(line, 2, row_count)[slot_pair]
    places = jnp.stack([places[:, x], places[:, 1 - x]], axis=1).reshape(1, total_rows)
    first = x * half + z * width
    taps = lax.dynamic_slice_in_dim(filters, first, width, 0).astype(jnp.float32)
    skip = lax.dynamic_slice_in_dim(skip_gain, first, width, 0)[None]
    flags = doc_flags(lengths, total_rows // filters.shape[1], jnp.float32)
    row_first = (z * width)[None].astype(jnp.int32)
    tall = half + EXTRA
    wide = 2 * row_count

    def projected(number, some):
        return project(which, weights, number, some, row_count)

    def scaled(arrays):
        return scale(picks, gains, half, arrays)

    def to_near(arrays):
        stacked = jnp.concatenate(arrays, axis=0) if len(arrays) > 1 else arrays[0]
        return to_owner(stacked, near_owner)

    def tie(*arrays):
        return lax.optimization_barrier(arrays)

    by_far, by_near = to_pair(tokens, far_pair), to_pair(tokens, near_pair)
    kept0, give0 = halve(which, tokens)
    got0, kept0_far = across(give0), to_owner(kept0, far_owner)
    got0_far = to_owner(got0, far_owner)
    most0 = jnp.concatenate([kept0, got0, kept0_far, got0_far], axis=0)
    packed_weights = pack_weights(give0, [w_value, w_gate], line)
    packed_weights, by_near = tie(packed_weights, by_near)
    kept1, give1 = halve(which, by_near)
    small = picks, gains, taps, skip, flags, row_first, places, which
    by_both = to_pair(by_far, near_pair)
    by_far, got0, kept0_far, got0_far, most0, kept1, give1, small, packed_weights = tie(
        by_far, got0, kept0_far, got0_far, most0, kept1, give1, small, packed_weights
    )
    picks, gains, taps, skip, flags, row_first, places, which = small

    kept2, give2 = halve(which, by_far)
    got1, kept1_far = across(give1), to_owner(kept1, far_owner)
    got2, kept2_far = across(give2), to_owner(kept2, far_owner)
    got1_far = to_owner(got1, far_owner)
    weights = along_line(packed_weights)
    by_both, got1, kept1_far, got1_far, got2, kept2_far = tie(
        by_both, got1, kept1_far, got1_far, got2, kept2_far
    )

    kept3, give3 = halve(which, by_both)
    got3, kept3_far = across(give3), to_owner(kept3, far_owner)
    got2_far = to_owner(got2, far_owner)
    all1 = to_near([kept1, got1, kept1_far, got1_far])
    all0 = to_near([most0])
    got3, kept3_far, got2_far, all0, all1 = tie(got3, kept3_far, got2_far, all0, all1)

    got3_far = to_owner(got3, far_owner)
    all2 = to_near([kept2, got2, kept2_far, got2_far])
    near_kept3, near_kept3_far, near_got3 = [to_near([some]) for some in (kept3, kept3_far, got3)]
    normed0 = scaled([kept0, got0, kept0_far, got0_far, all0])
    normed1 = scaled([kept1, got1, kept1_far, got1_far, all1])
    got3_far, all2, near_kept3, near_kept3_far, near_got3, normed0, normed1 = tie(
        got3_far, all2, near_kept3, near_kept3_far, near_got3, normed0, normed1
    )

    near_got3_far = to_near([got3_far])
    normed2 = scaled([kept2, got2, kept2_far, got2_far, all2])
    near_got3_far, normed2 = tie(near_got3_far, normed2)
    normed3 = scaled(
        [kept3, got3, kept3_far, got3_far, near_kept3, near_got3, near_kept3_far, near_got3_far]
    )
    normed3, weights = tie(normed3, weights)

    cut = 2 * wide
    value0, far0 = projected(0, [normed0, normed1])
    theirs0 = across(far0)
    value0, normed2 = tie(value0, normed2)
    value2, far2 = projected(0, [normed2, normed3])
    theirs2 = across(far2)
    normed0, value2 = tie(normed0, value2)
    gate0, gate_far0 = projected(1, [normed0, normed1])
    gate2, gate_far2 = projected(1, [normed2, normed3])
    early = place(
        row_first, total_rows, value0, theirs0, places[:, :cut], tall, [kept0, got0, kept1, got1]
    )
    early, theirs2, gate_far0, gate_far2 = tie(early, theirs2, gate_far0, gate_far2)
    gate_theirs0, gate_theirs2 = across(gate_far0), across(gate_far2)
    banded, packed = band_of(
        flags, row_first, taps, skip, early, value2, theirs2, places[:, cut:], tall,
        [kept2, got2, kept3, got3],
    )
    early = place(row_first, total_rows, gate0, gate_theirs0, places[:, :cut])
    mixed = mix(banded, packed, early, gate2, gate_theirs2, places[:, cut:], shards)
    owners = [[number(zz, xx, mm) for xx in range(2) for zz in range(line)] for mm in range(groups)]
    mixed = lax.all_to_all(
        mixed, AXES, split_axis=0, concat_axis=0, tiled=True, axis_index_groups=owners
    )
    return mixed.reshape(features, row_count)


def solution(mesh):
    placed = (P("mp", "seq"), P(), P(), P("seq", "mp"), P("seq", "mp"), P("mp", None), P("mp"), P())
    shards, groups = mesh.shape["seq"], mesh.shape["mp"]

    def whole(*args):
        tokens, w_value, filters = args[0], args[3], args[5]
        moves_tokens = (
            tokens.shape[1] <= w_value.shape[1]
            and shards == 2 * groups
            and groups & (groups - 1) == 0
            and (groups - 1).bit_count() == 2
            and tokens.shape[0] % (LANES * shards * groups) == 0
            and filters.shape[1] % LANES == 0
            and tokens.shape[1] // shards % filters.shape[1] == 0
        )
        body = on_device_line if moves_tokens else on_device
        return jax.shard_map(
            body, mesh=mesh, in_specs=placed, out_specs=P("mp", "seq"), check_vma=False
        )(*args)

    return whole
```

```python
import functools
import math

import jax
import jax.numpy as jnp
from jax import lax
from jax.experimental import pallas as pl
from jax.experimental.pallas import tpu as pltpu
from jax.sharding import PartitionSpec as P

epsilon = 1e-05
AXES = ("seq", "mp")
LANES = 128
SUBLANES = 8
EXTRA = 2 * SUBLANES
VMEM = pl.BlockSpec(memory_space=pltpu.VMEM)
ANY = pl.BlockSpec(memory_space=pl.ANY)
SMEM = pl.BlockSpec(memory_space=pltpu.SMEM)
PARAMS = pltpu.CompilerParams(vmem_limit_bytes=16 * 1024 * 1024)


def toeplitz(filter_taps):
    chan_count, tap_count = filter_taps.shape
    padding = jnp.zeros((chan_count, tap_count), filter_taps.dtype)
    line_row = jnp.concatenate([padding, filter_taps[:, ::-1], padding], axis=1)
    tiled = jnp.tile(line_row, (1, tap_count))[:, : tap_count * (3 * tap_count - 1)]
    return tiled.reshape(chan_count, tap_count, 3 * tap_count - 1)[
        :, :, tap_count - 1 : 3 * tap_count - 1
    ]


def doc_flags(lengths, block_count, dtype):
    starts = jnp.cumsum(lengths, dtype=jnp.int32) - lengths
    block_index = jnp.arange(block_count, dtype=jnp.int32)
    is_start = jnp.any(block_index[:, None] == starts[None, :], axis=1)
    return jnp.where(is_start, 0.0, 1.0).astype(dtype)


def band_product(values, prior_rim, filter_taps, link_flags):
    chan_count, seq_length = values.shape
    tap_count = filter_taps.shape[1]
    block_count = seq_length // tap_count
    group_size = math.gcd(chan_count, 64)
    groups = chan_count // group_size

    def one_group(group_args):
        part_values, part_rim, part_taps = group_args
        blocks = part_values.reshape(group_size, block_count, tap_count)
        earlier = jnp.concatenate([part_rim[:, None, :], blocks[:, :-1, :]], axis=1)
        earlier = earlier * link_flags[None, :, None]
        joined = jnp.concatenate([earlier, blocks], axis=2)
        banded = jnp.einsum(
            "cpq,cbq->cbp", toeplitz(part_taps), joined, preferred_element_type=jnp.float32
        )
        return banded.reshape(group_size, seq_length)

    result = lax.map(
        one_group,
        (
            values.reshape(groups, group_size, seq_length),
            prior_rim.reshape(groups, group_size, tap_count),
            filter_taps.reshape(groups, group_size, tap_count),
        ),
    )
    return result.reshape(chan_count, seq_length)


def project_all(all_features, norm_gain, weight_pair):
    widened = all_features.astype(jnp.float32)
    inv_scale = lax.rsqrt(jnp.mean(widened * widened, axis=0, keepdims=True) + epsilon)
    normed = (widened * inv_scale * norm_gain[:, None]).astype(jnp.bfloat16)
    contract = (((0,), (0,)), ((), ()))
    value_part = lax.dot_general(
        weight_pair[0], normed, contract, preferred_element_type=jnp.float32
    ).astype(jnp.bfloat16)
    gate_part = lax.dot_general(
        weight_pair[1], normed, contract, preferred_element_type=jnp.float32
    ).astype(jnp.bfloat16)
    return (value_part, gate_part)


def on_device(tokens, packing, norm_gain, w_value, w_gate, filters, skip_gain, lengths):
    row_count = tokens.shape[1]
    shards = lax.axis_size("seq")
    my_index = lax.axis_index("seq")
    all_count = packing.shape[0]
    tap_count = filters.shape[1]
    chan_count = tokens.shape[0] // shards
    weight_pair = (
        lax.all_gather(w_value, "seq", axis=0, tiled=True),
        lax.all_gather(w_gate, "seq", axis=0, tiled=True),
    )
    inverse = (
        jnp.zeros((all_count,), jnp.int32).at[packing].set(jnp.arange(all_count, dtype=jnp.int32))
    )
    chan_taps = lax.dynamic_slice_in_dim(filters, my_index * chan_count, chan_count, 0)
    chan_skip = lax.dynamic_slice_in_dim(skip_gain, my_index * chan_count, chan_count, 0)
    slot_cap = 2 * (row_count // shards)
    own_packing = lax.dynamic_slice_in_dim(packing, my_index * row_count, row_count)
    dest_owner = own_packing // row_count
    onehot = (dest_owner[:, None] == jnp.arange(shards, dtype=jnp.int32)[None, :]).astype(jnp.int32)
    slot_rank = jnp.sum((jnp.cumsum(onehot, axis=0, dtype=jnp.int32) - onehot) * onehot, axis=1)
    slot_index = dest_owner * slot_cap + slot_rank
    send_buffer = (
        jnp.zeros((tokens.shape[0], shards * slot_cap), jnp.bfloat16).at[:, slot_index].set(tokens)
    )
    received = lax.all_to_all(send_buffer, "seq", split_axis=1, concat_axis=1, tiled=True)
    my_sources = lax.dynamic_slice_in_dim(inverse, my_index * row_count, row_count)
    to_me = (packing // row_count == my_index).astype(jnp.int32).reshape(shards, row_count)
    arrival_rank = (jnp.cumsum(to_me, axis=1, dtype=jnp.int32) - to_me).reshape(all_count)
    packed = received[:, my_sources // row_count * slot_cap + arrival_rank[my_sources]]
    all_features = lax.all_gather(packed, "mp", axis=0, tiled=True)
    value_part, gate_part = project_all(all_features, norm_gain, weight_pair)
    value_chan = lax.all_to_all(value_part, "seq", split_axis=0, concat_axis=1, tiled=True)
    link_flags = doc_flags(lengths, all_count // tap_count, jnp.bfloat16)
    prior_rim = jnp.zeros((chan_count, tap_count), jnp.bfloat16)
    banded = band_product(value_chan, prior_rim, chan_taps, link_flags)
    chan_band = (banded + chan_skip[:, None] * value_chan.astype(jnp.float32)).astype(jnp.bfloat16)
    mixed_band = lax.all_to_all(chan_band, "seq", split_axis=1, concat_axis=0, tiled=True)
    mixed_band = lax.optimization_barrier(mixed_band)
    gate_wide = lax.optimization_barrier(gate_part).astype(jnp.float32)
    return (packed.astype(jnp.float32) + gate_wide * mixed_band.astype(jnp.float32)).astype(
        jnp.bfloat16
    )


def halve_kernel(x_ref, token_ref, keep_ref, give_ref):
    features, count = token_ref.shape
    half = features // 2
    x = x_ref[0]
    widened = token_ref[...].astype(jnp.float32)
    rest = jnp.sum(widened * widened, axis=0, keepdims=True)
    terms = []
    for _ in range(3):
        term = rest.astype(jnp.bfloat16).astype(jnp.float32)
        terms.append(term)
        rest = rest - term
    row = lax.broadcasted_iota(jnp.int32, (EXTRA, count), 0)
    extra = jnp.zeros(row.shape, jnp.float32)
    for i, term in enumerate(terms):
        extra = jnp.where(row == i, term, extra)
    extra = extra.astype(jnp.bfloat16)
    for out_ref, which in ((keep_ref, x), (give_ref, 1 - x)):
        out_ref[0:half, :] = token_ref[pl.ds(pl.multiple_of(which * half, half), half), :]
        out_ref[half : half + EXTRA, :] = extra


def halve(x, tokens):
    features, count = tokens.shape
    out = jax.ShapeDtypeStruct((features // 2 + EXTRA, count), tokens.dtype)
    return pl.pallas_call(
        halve_kernel,
        out_shape=[out, out],
        in_specs=[SMEM, VMEM],
        out_specs=[VMEM, VMEM],
        compiler_params=PARAMS,
        cost_estimate=pl.CostEstimate(
            flops=2 * features * count, bytes_accessed=4 * features * count, transcendentals=0
        ),
    )(x, tokens)


def pack_kernel(after_ref, *refs):
    out_ref = refs[-1]
    line, _, _, width, _ = out_ref.shape
    for which, ref in enumerate(refs[:-1]):
        for target in range(line):
            for half in range(2):
                first = (half * line + target) * width
                out_ref[target, which, half] = ref[:, first : first + width].T


def pack_weights(after, weights, line):
    height, columns = weights[0].shape
    out = (line, len(weights), 2, columns // (2 * line), height)
    return pl.pallas_call(
        pack_kernel,
        out_shape=jax.ShapeDtypeStruct(out, weights[0].dtype),
        in_specs=[ANY] + [VMEM] * len(weights),
        out_specs=VMEM,
        compiler_params=PARAMS,
        cost_estimate=pl.CostEstimate(
            flops=0, bytes_accessed=4 * height * columns * len(weights), transcendentals=0
        ),
    )(after, *weights)


def scale_kernel(height, pick_ref, gain_ref, *refs):
    arrays, out_ref = refs[:-1], refs[-1]
    parts = out_ref.shape[0]
    tall = height + EXTRA
    blocks = [
        ref.at[first : first + tall] for ref in arrays for first in range(0, ref.shape[0], tall)
    ]
    each = len(blocks) // parts
    count = out_ref.shape[2] // each
    slots = each // 2 if each > 1 else 1
    features = 2 * height * parts
    gain_columns = gain_ref[...].T
    for number in range(each):
        slot, half = number % slots, number // slots
        first = (slot * (each // slots) + half) * count
        squares = jnp.zeros((1, count), jnp.float32)
        for block in blocks[number::each]:
            terms = block[height:tall, :].astype(jnp.float32)
            squares += jnp.sum(terms, axis=0, keepdims=True)
        inv_row = lax.rsqrt(squares / features + epsilon)
        for part in range(parts):
            scaled = blocks[part * each + number][0:height, :].astype(jnp.float32) * inv_row
            scaled = (scaled * gain_columns[:, part : part + 1]).astype(jnp.bfloat16)
            out_ref[pick_ref[part], :, first : first + count] = scaled


def scale(picks, gains, height, arrays):
    parts = picks.shape[0]
    count = arrays[0].shape[1]
    each = sum(array.shape[0] for array in arrays) // (height + EXTRA) // parts
    return pl.pallas_call(
        functools.partial(scale_kernel, height),
        out_shape=jax.ShapeDtypeStruct((parts, height, count * each), jnp.bfloat16),
        in_specs=[SMEM] + [VMEM] * (1 + len(arrays)),
        out_specs=VMEM,
        compiler_params=PARAMS,
        cost_estimate=pl.CostEstimate(
            flops=2 * parts * height * count * each,
            bytes_accessed=4 * parts * height * count * each,
            transcendentals=0,
        ),
    )(picks, gains, *arrays)


def project_kernel(number, row_count, x_ref, weight_ref, *refs):
    mine_ref, other_ref = refs[-2:]
    x = x_ref[0]
    first = 0
    for ref in refs[:-2]:
        parts, _, count = ref.shape
        mine = jnp.zeros((mine_ref.shape[0], count), jnp.float32)
        other = jnp.zeros((mine_ref.shape[0], count), jnp.float32)
        for part in range(parts):
            block = ref[part]
            mine += jnp.dot(
                weight_ref[part, number, x], block, preferred_element_type=jnp.float32
            )
            other += jnp.dot(
                weight_ref[part, number, 1 - x], block, preferred_element_type=jnp.float32
            )
        mine_ref[:, first : first + count] = mine
        other = other.astype(jnp.bfloat16)
        other_ref[:, first : first + row_count] = other[:, row_count:]
        other_ref[:, first + row_count : first + count] = other[:, :row_count]
        first += count


def project(x, weights, number, normed, row_count):
    line, _, _, width, height = weights.shape
    out = (width, sum(some.shape[2] for some in normed))
    return pl.pallas_call(
        functools.partial(project_kernel, number, row_count),
        out_shape=[
            jax.ShapeDtypeStruct(out, jnp.float32),
            jax.ShapeDtypeStruct(out, jnp.bfloat16),
        ],
        in_specs=[SMEM] + [VMEM] * (1 + len(normed)),
        out_specs=[VMEM, VMEM],
        compiler_params=PARAMS,
        cost_estimate=pl.CostEstimate(
            flops=4 * width * height * out[1] * line,
            bytes_accessed=weights.size + 2 * height * out[1] * line,
            transcendentals=0,
        ),
    )(x, weights, *normed)


def column_of(row):
    tall = jnp.broadcast_to(row.astype(jnp.float32), (SUBLANES, row.shape[1])).T
    return tall[:, 0:1].astype(row.dtype)


def at_places(array, place_row, total):
    spot = lax.broadcasted_iota(jnp.int32, (array.shape[1], total), 1)
    onehot = (column_of(place_row) == spot).astype(jnp.float32).astype(jnp.bfloat16)
    return jnp.dot(array, onehot, preferred_element_type=jnp.float32)


def with_tokens(first, tall, summed, token_refs):
    chan = summed.shape[0]
    first = pl.multiple_of(first, chan)
    tokens = []
    for kept_ref, got_ref in zip(token_refs[::2], token_refs[1::2]):
        for start in range(0, kept_ref.shape[0], tall):
            tokens += [ref[pl.ds(first + start, chan), :] for ref in (kept_ref, got_ref)]
    return jnp.concatenate([summed, jnp.concatenate(tokens, axis=1)], axis=0)


def place_kernel(tall, many, first_ref, mine_ref, theirs_ref, place_ref, *refs):
    tokens, before, out_ref = refs[:many], refs[many:-1], refs[-1]
    count = place_ref.shape[1]
    summed = mine_ref[:, :count] + theirs_ref[:, :count].astype(jnp.float32)
    summed = summed.astype(jnp.bfloat16)
    if tokens:
        summed = with_tokens(first_ref[0], tall, summed, tokens)
    moved = at_places(summed, place_ref[...], out_ref.shape[1])
    for ref in before:
        moved += ref[...].astype(jnp.float32)
    out_ref[...] = moved.astype(jnp.bfloat16)


def place(first, total, mine, theirs, places, tall=0, tokens=(), before=()):
    chan, count = mine.shape[0], places.shape[1]
    return pl.pallas_call(
        functools.partial(place_kernel, tall, len(tokens)),
        out_shape=jax.ShapeDtypeStruct((2 * chan if tokens else chan, total), jnp.bfloat16),
        in_specs=[SMEM] + [VMEM] * (3 + len(tokens) + len(before)),
        out_specs=VMEM,
        compiler_params=PARAMS,
        cost_estimate=pl.CostEstimate(
            flops=2 * chan * total * count, bytes_accessed=8 * chan * total, transcendentals=0
        ),
    )(first, mine, theirs, places, *tokens, *before)


def band_kernel(
    taps_blocks, tall, flag_ref, first_ref, taps_ref, skip_ref, early_ref, mine_ref, theirs_ref,
    last_mine_ref, last_theirs_ref, place_ref, *refs
):
    shifted = refs[-taps_blocks - 1 :]
    out_ref, packed_ref, whole, band = refs[-taps_blocks - 5 : -taps_blocks - 1]
    chan = taps_ref.shape[0]
    total = whole.shape[1]
    pieces = total // LANES
    summed = jnp.concatenate(
        [
            (mine[...] + theirs[...].astype(jnp.float32)).astype(jnp.bfloat16)
            for mine, theirs in ((mine_ref, theirs_ref), (last_mine_ref, last_theirs_ref))
        ],
        axis=1,
    )
    summed = with_tokens(first_ref[0], tall, summed, refs[: -taps_blocks - 5])
    moved = at_places(summed, place_ref[...], total) + early_ref[...].astype(jnp.float32)
    whole[...] = moved[0:chan]
    packed_ref[...] = moved[chan : 2 * chan].astype(jnp.bfloat16)
    for piece in range(pieces):
        for back in range(taps_blocks + 1):
            rows = pl.ds(piece * chan, chan)
            if back > piece:
                shifted[back][rows, :] = jnp.zeros((chan, LANES), jnp.float32)
                continue
            first = (piece - back) * LANES
            part = whole[:, first : first + LANES]
            if back > piece % taps_blocks:
                part = part * flag_ref[piece // taps_blocks]
            shifted[back][rows, :] = part
    column = lax.broadcasted_iota(jnp.int32, (LANES, LANES), 1).astype(jnp.bfloat16)
    row = lax.broadcasted_iota(jnp.int32, (LANES, LANES), 0).astype(jnp.bfloat16)
    later = column >= row
    zero = jnp.zeros((LANES, LANES), jnp.bfloat16)

    def one(group, carry):
        base = pl.multiple_of(group * SUBLANES, SUBLANES)
        group_taps = taps_ref[pl.ds(base, SUBLANES), :]
        for member in range(SUBLANES):
            turned = [zero]
            for block in range(taps_blocks):
                line_row = group_taps[member : member + 1, block * LANES : (block + 1) * LANES]
                square = jnp.broadcast_to(line_row, (LANES, LANES))
                square = pltpu.roll(square, 0, 1, stride=1, stride_axis=0)
                turned.append(square.astype(jnp.bfloat16))
            turned.append(zero)
            rows = pl.ds(base + member, pieces, stride=chan)
            tiles, inputs = [], []
            for back in range(taps_blocks + 1):
                tiles.append(jnp.where(later, turned[back + 1], turned[back]))
                inputs.append(shifted[back][rows, :].astype(jnp.bfloat16))
            band[rows, :] = jnp.dot(
                jnp.concatenate(inputs, axis=1),
                jnp.concatenate(tiles, axis=0),
                preferred_element_type=jnp.float32,
            )
        return carry

    lax.fori_loop(0, chan // SUBLANES, one, 0, unroll=4)
    skip = column_of(skip_ref[...])
    for piece in range(pieces):
        lanes = slice(piece * LANES, (piece + 1) * LANES)
        rows = pl.ds(piece * chan, chan)
        out_ref[:, lanes] = (band[rows, :] + skip * whole[:, lanes]).astype(jnp.bfloat16)


def band_of(flags, first, taps, skip, early, late, last, places, tall, tokens):
    chan, tap_count = taps.shape
    total = early.shape[1]
    taps_blocks = tap_count // LANES
    tower = (total // LANES * chan, LANES)
    out = jax.ShapeDtypeStruct((chan, total), jnp.bfloat16)
    return pl.pallas_call(
        functools.partial(band_kernel, taps_blocks, tall),
        out_shape=[out, out],
        in_specs=[SMEM, SMEM] + [VMEM] * (8 + len(tokens)),
        out_specs=[VMEM, VMEM],
        scratch_shapes=[pltpu.VMEM((chan, total), jnp.float32)]
        + [pltpu.VMEM(tower, jnp.float32)] * (taps_blocks + 2),
        compiler_params=PARAMS,
        cost_estimate=pl.CostEstimate(
            flops=3 * chan * total * total, bytes_accessed=16 * chan * total, transcendentals=0
        ),
    )(flags, first, taps, skip, early, *late, *last, places, *tokens)


def mix_kernel(z_ref, packed_ref, early_ref, mine_ref, theirs_ref, place_ref, out_ref):
    summed = (mine_ref[...] + theirs_ref[...].astype(jnp.float32)).astype(jnp.bfloat16)
    gate = at_places(summed, place_ref[...], z_ref.shape[1]) + early_ref[...].astype(jnp.float32)
    mixed = packed_ref[...].astype(jnp.float32) + gate * z_ref[...].astype(jnp.float32)
    mixed = mixed.astype(jnp.bfloat16)
    wide = out_ref.shape[2]
    pairs = out_ref.shape[0] // 2
    for place in range(2 * pairs):
        owner = place % pairs * 2 + place // pairs
        out_ref[place] = mixed[:, owner * wide : (owner + 1) * wide]


def mix(z, packed, early, mine, theirs, places, shards):
    chan, total = z.shape
    return pl.pallas_call(
        mix_kernel,
        out_shape=jax.ShapeDtypeStruct((shards, chan, total // shards), jnp.bfloat16),
        in_specs=[VMEM] * 6,
        out_specs=VMEM,
        compiler_params=PARAMS,
        cost_estimate=pl.CostEstimate(
            flops=chan * total * total, bytes_accessed=16 * chan * total, transcendentals=0
        ),
    )(z, packed, early, mine, theirs, places)


def on_device_line(tokens, packing, norm_gain, w_value, w_gate, filters, skip_gain, lengths):
    shards, groups = lax.axis_size("seq"), lax.axis_size("mp")
    line = shards // 2
    s, m = lax.axis_index("seq"), lax.axis_index("mp")
    z, x = s // 2, s % 2
    features, row_count = tokens.shape
    half = features // 2
    total_rows = packing.shape[0]
    width = features // shards

    def number(zz, xx, mm):
        return (zz * 2 + xx) * groups + mm

    def send(array, target):
        pairs = []
        for zz in range(line):
            for xx in range(2):
                for mm in range(groups):
                    to = target(zz, xx, mm)
                    if to is not None:
                        pairs.append((number(zz, xx, mm), number(*to)))
        return lax.ppermute(array, AXES, pairs)

    def across(array):
        return send(array, lambda zz, xx, mm: (zz, 1 - xx, mm))

    def to_owner(array, o):
        return send(array, lambda zz, xx, mm: (zz, xx, mm ^ o))

    columns = [[number(zz, xx, mm) for zz in range(line)] for xx in range(2) for mm in range(groups)]

    def along_line(array):
        return lax.all_to_all(
            array, AXES, split_axis=0, concat_axis=0, tiled=True, axis_index_groups=columns
        )

    def to_pair(array, o):
        return send(array, lambda zz, xx, mm: (zz ^ o, xx, mm))

    slot_pair = jnp.stack([z ^ o for o in range(line)])
    far_owner, near_owner, far_pair, near_pair = groups // 2, groups // 4, line // 2, line // 4
    owners = jnp.stack([m ^ o for o in (0, far_owner, near_owner, far_owner ^ near_owner)])
    which = x[None].astype(jnp.int32)
    picks = owners.astype(jnp.int32)
    gains = norm_gain.reshape(groups, 2, half)[:, x][owners]
    gains = jnp.pad(gains, ((0, -groups % SUBLANES), (0, 0)))
    places = packing.reshape(line, 2, row_count)[slot_pair]
    places = jnp.stack([places[:, x], places[:, 1 - x]], axis=1).reshape(1, total_rows)
    first = x * half + z * width
    taps = lax.dynamic_slice_in_dim(filters, first, width, 0).astype(jnp.float32)
    skip = lax.dynamic_slice_in_dim(skip_gain, first, width, 0)[None]
    flags = doc_flags(lengths, total_rows // filters.shape[1], jnp.float32)
    row_first = (z * width)[None].astype(jnp.int32)
    tall = half + EXTRA
    wide = 2 * row_count

    def projected(number, some):
        return project(which, weights, number, some, row_count)

    def scaled(arrays):
        return scale(picks, gains, half, arrays)

    def to_near(arrays):
        stacked = jnp.concatenate(arrays, axis=0) if len(arrays) > 1 else arrays[0]
        return to_owner(stacked, near_owner)

    def tie(*arrays):
        return lax.optimization_barrier(arrays)

    by_far, by_near = to_pair(tokens, far_pair), to_pair(tokens, near_pair)
    kept0, give0 = halve(which, tokens)
    got0, kept0_far = across(give0), to_owner(kept0, far_owner)
    got0_far = to_owner(got0, far_owner)
    most0 = jnp.concatenate([kept0, got0, kept0_far, got0_far], axis=0)
    packed_weights = pack_weights(give0, [w_value, w_gate], line)
    packed_weights, by_near, most0 = tie(packed_weights, by_near, most0)
    kept1, give1 = halve(which, by_near)
    small = picks, gains, taps, skip, flags, row_first, places, which
    by_both = to_pair(by_far, near_pair)
    by_far, got0, kept0_far, got0_far, most0, kept1, give1, small, packed_weights = tie(
        by_far, got0, kept0_far, got0_far, most0, kept1, give1, small, packed_weights
    )
    picks, gains, taps, skip, flags, row_first, places, which = small

    kept2, give2 = halve(which, by_far)
    got1, kept1_far = across(give1), to_owner(kept1, far_owner)
    got2, kept2_far = across(give2), to_owner(kept2, far_owner)
    got1_far = to_owner(got1, far_owner)
    weights = along_line(packed_weights)
    by_both, got1, kept1_far, got1_far, got2, kept2_far = tie(
        by_both, got1, kept1_far, got1_far, got2, kept2_far
    )

    kept3, give3 = halve(which, by_both)
    got3, kept3_far = across(give3), to_owner(kept3, far_owner)
    got2_far = to_owner(got2, far_owner)
    all1 = to_near([kept1, got1, kept1_far, got1_far])
    all0 = to_near([most0])
    got3, kept3_far, got2_far, all0, all1 = tie(got3, kept3_far, got2_far, all0, all1)

    got3_far = to_owner(got3, far_owner)
    all2 = to_near([kept2, got2, kept2_far, got2_far])
    near_kept3, near_kept3_far, near_got3 = [to_near([some]) for some in (kept3, kept3_far, got3)]
    normed0 = scaled([kept0, got0, kept0_far, got0_far, all0])
    normed1 = scaled([kept1, got1, kept1_far, got1_far, all1])
    got3_far, all2, near_kept3, near_kept3_far, near_got3, normed0, normed1 = tie(
        got3_far, all2, near_kept3, near_kept3_far, near_got3, normed0, normed1
    )

    near_got3_far = to_near([got3_far])
    normed2 = scaled([kept2, got2, kept2_far, got2_far, all2])
    near_got3_far, normed2 = tie(near_got3_far, normed2)
    normed3 = scaled(
        [kept3, got3, kept3_far, got3_far, near_kept3, near_got3, near_kept3_far, near_got3_far]
    )
    normed3, weights = tie(normed3, weights)

    value0, far0 = projected(0, [normed0])
    theirs0 = across(far0)
    value0, normed1 = tie(value0, normed1)
    value1, far1 = projected(0, [normed1, normed2])
    theirs1 = across(far1)
    value1, normed3, theirs0 = tie(value1, normed3, theirs0)
    value3, far3 = projected(0, [normed3])
    theirs3 = across(far3)
    normed0, normed3, value3 = tie(normed0, normed3, value3)
    gate0, gate_far0 = projected(1, [normed0, normed1])
    gate2, gate_far2 = projected(1, [normed2, normed3])
    early = place(
        row_first, total_rows, value0, theirs0, places[:, :wide], tall, [kept0, got0]
    )
    theirs1, gate_far0, gate_far2 = tie(theirs1, gate_far0, gate_far2)
    gate_theirs0, gate_theirs2 = across(gate_far0), across(gate_far2)
    banded, packed = band_of(
        flags, row_first, taps, skip, early, (value1, theirs1), (value3, theirs3),
        places[:, wide:], tall, [kept1, got1, kept2, got2, kept3, got3],
    )
    cut = 2 * wide
    early = place(row_first, total_rows, gate0, gate_theirs0, places[:, :cut])
    mixed = mix(banded, packed, early, gate2, gate_theirs2, places[:, cut:], shards)
    owners = [[number(zz, xx, mm) for xx in range(2) for zz in range(line)] for mm in range(groups)]
    mixed = lax.all_to_all(
        mixed, AXES, split_axis=0, concat_axis=0, tiled=True, axis_index_groups=owners
    )
    return mixed.reshape(features, row_count)


def solution(mesh):
    placed = (P("mp", "seq"), P(), P(), P("seq", "mp"), P("seq", "mp"), P("mp", None), P("mp"), P())
    shards, groups = mesh.shape["seq"], mesh.shape["mp"]

    def whole(*args):
        tokens, w_value, filters = args[0], args[3], args[5]
        moves_tokens = (
            tokens.shape[1] <= w_value.shape[1]
            and shards == 2 * groups
            and groups & (groups - 1) == 0
            and (groups - 1).bit_count() == 2
            and tokens.shape[0] % (LANES * shards * groups) == 0
            and filters.shape[1] % LANES == 0
            and tokens.shape[1] // shards % filters.shape[1] == 0
        )
        body = on_device_line if moves_tokens else on_device
        return jax.shard_map(
            body, mesh=mesh, in_specs=placed, out_specs=P("mp", "seq"), check_vma=False
        )(*args)

    return whole
```

```python
import functools
import math

import jax
import jax.numpy as jnp
from jax import lax
from jax.experimental import pallas as pl
from jax.experimental.pallas import tpu as pltpu
from jax.sharding import PartitionSpec as P

epsilon = 1e-05
AXES = ("seq", "mp")
LANES = 128
SUBLANES = 8
EXTRA = 2 * SUBLANES
VMEM = pl.BlockSpec(memory_space=pltpu.VMEM)
ANY = pl.BlockSpec(memory_space=pl.ANY)
SMEM = pl.BlockSpec(memory_space=pltpu.SMEM)
PARAMS = pltpu.CompilerParams(vmem_limit_bytes=16 * 1024 * 1024)


def toeplitz(filter_taps):
    chan_count, tap_count = filter_taps.shape
    padding = jnp.zeros((chan_count, tap_count), filter_taps.dtype)
    line_row = jnp.concatenate([padding, filter_taps[:, ::-1], padding], axis=1)
    tiled = jnp.tile(line_row, (1, tap_count))[:, : tap_count * (3 * tap_count - 1)]
    return tiled.reshape(chan_count, tap_count, 3 * tap_count - 1)[
        :, :, tap_count - 1 : 3 * tap_count - 1
    ]


def doc_flags(lengths, block_count, dtype):
    starts = jnp.cumsum(lengths, dtype=jnp.int32) - lengths
    block_index = jnp.arange(block_count, dtype=jnp.int32)
    is_start = jnp.any(block_index[:, None] == starts[None, :], axis=1)
    return jnp.where(is_start, 0.0, 1.0).astype(dtype)


def band_product(values, prior_rim, filter_taps, link_flags):
    chan_count, seq_length = values.shape
    tap_count = filter_taps.shape[1]
    block_count = seq_length // tap_count
    group_size = math.gcd(chan_count, 64)
    groups = chan_count // group_size

    def one_group(group_args):
        part_values, part_rim, part_taps = group_args
        blocks = part_values.reshape(group_size, block_count, tap_count)
        earlier = jnp.concatenate([part_rim[:, None, :], blocks[:, :-1, :]], axis=1)
        earlier = earlier * link_flags[None, :, None]
        joined = jnp.concatenate([earlier, blocks], axis=2)
        banded = jnp.einsum(
            "cpq,cbq->cbp", toeplitz(part_taps), joined, preferred_element_type=jnp.float32
        )
        return banded.reshape(group_size, seq_length)

    result = lax.map(
        one_group,
        (
            values.reshape(groups, group_size, seq_length),
            prior_rim.reshape(groups, group_size, tap_count),
            filter_taps.reshape(groups, group_size, tap_count),
        ),
    )
    return result.reshape(chan_count, seq_length)


def project_all(all_features, norm_gain, weight_pair):
    widened = all_features.astype(jnp.float32)
    inv_scale = lax.rsqrt(jnp.mean(widened * widened, axis=0, keepdims=True) + epsilon)
    normed = (widened * inv_scale * norm_gain[:, None]).astype(jnp.bfloat16)
    contract = (((0,), (0,)), ((), ()))
    value_part = lax.dot_general(
        weight_pair[0], normed, contract, preferred_element_type=jnp.float32
    ).astype(jnp.bfloat16)
    gate_part = lax.dot_general(
        weight_pair[1], normed, contract, preferred_element_type=jnp.float32
    ).astype(jnp.bfloat16)
    return (value_part, gate_part)


def on_device(tokens, packing, norm_gain, w_value, w_gate, filters, skip_gain, lengths):
    row_count = tokens.shape[1]
    shards = lax.axis_size("seq")
    my_index = lax.axis_index("seq")
    all_count = packing.shape[0]
    tap_count = filters.shape[1]
    chan_count = tokens.shape[0] // shards
    weight_pair = (
        lax.all_gather(w_value, "seq", axis=0, tiled=True),
        lax.all_gather(w_gate, "seq", axis=0, tiled=True),
    )
    inverse = (
        jnp.zeros((all_count,), jnp.int32).at[packing].set(jnp.arange(all_count, dtype=jnp.int32))
    )
    chan_taps = lax.dynamic_slice_in_dim(filters, my_index * chan_count, chan_count, 0)
    chan_skip = lax.dynamic_slice_in_dim(skip_gain, my_index * chan_count, chan_count, 0)
    slot_cap = 2 * (row_count // shards)
    own_packing = lax.dynamic_slice_in_dim(packing, my_index * row_count, row_count)
    dest_owner = own_packing // row_count
    onehot = (dest_owner[:, None] == jnp.arange(shards, dtype=jnp.int32)[None, :]).astype(jnp.int32)
    slot_rank = jnp.sum((jnp.cumsum(onehot, axis=0, dtype=jnp.int32) - onehot) * onehot, axis=1)
    slot_index = dest_owner * slot_cap + slot_rank
    send_buffer = (
        jnp.zeros((tokens.shape[0], shards * slot_cap), jnp.bfloat16).at[:, slot_index].set(tokens)
    )
    received = lax.all_to_all(send_buffer, "seq", split_axis=1, concat_axis=1, tiled=True)
    my_sources = lax.dynamic_slice_in_dim(inverse, my_index * row_count, row_count)
    to_me = (packing // row_count == my_index).astype(jnp.int32).reshape(shards, row_count)
    arrival_rank = (jnp.cumsum(to_me, axis=1, dtype=jnp.int32) - to_me).reshape(all_count)
    packed = received[:, my_sources // row_count * slot_cap + arrival_rank[my_sources]]
    all_features = lax.all_gather(packed, "mp", axis=0, tiled=True)
    value_part, gate_part = project_all(all_features, norm_gain, weight_pair)
    value_chan = lax.all_to_all(value_part, "seq", split_axis=0, concat_axis=1, tiled=True)
    link_flags = doc_flags(lengths, all_count // tap_count, jnp.bfloat16)
    prior_rim = jnp.zeros((chan_count, tap_count), jnp.bfloat16)
    banded = band_product(value_chan, prior_rim, chan_taps, link_flags)
    chan_band = (banded + chan_skip[:, None] * value_chan.astype(jnp.float32)).astype(jnp.bfloat16)
    mixed_band = lax.all_to_all(chan_band, "seq", split_axis=1, concat_axis=0, tiled=True)
    mixed_band = lax.optimization_barrier(mixed_band)
    gate_wide = lax.optimization_barrier(gate_part).astype(jnp.float32)
    return (packed.astype(jnp.float32) + gate_wide * mixed_band.astype(jnp.float32)).astype(
        jnp.bfloat16
    )


def halve_kernel(x_ref, token_ref, keep_ref, give_ref):
    features, count = token_ref.shape
    half = features // 2
    x = x_ref[0]
    widened = token_ref[...].astype(jnp.float32)
    rest = jnp.sum(widened * widened, axis=0, keepdims=True)
    terms = []
    for _ in range(3):
        term = rest.astype(jnp.bfloat16).astype(jnp.float32)
        terms.append(term)
        rest = rest - term
    row = lax.broadcasted_iota(jnp.int32, (EXTRA, count), 0)
    extra = jnp.zeros(row.shape, jnp.float32)
    for i, term in enumerate(terms):
        extra = jnp.where(row == i, term, extra)
    extra = extra.astype(jnp.bfloat16)
    for out_ref, which in ((keep_ref, x), (give_ref, 1 - x)):
        out_ref[0:half, :] = token_ref[pl.ds(pl.multiple_of(which * half, half), half), :]
        out_ref[half : half + EXTRA, :] = extra


def halve(x, tokens):
    features, count = tokens.shape
    out = jax.ShapeDtypeStruct((features // 2 + EXTRA, count), tokens.dtype)
    return pl.pallas_call(
        halve_kernel,
        out_shape=[out, out],
        in_specs=[SMEM, VMEM],
        out_specs=[VMEM, VMEM],
        compiler_params=PARAMS,
        cost_estimate=pl.CostEstimate(
            flops=2 * features * count, bytes_accessed=4 * features * count, transcendentals=0
        ),
    )(x, tokens)


def pack_kernel(after_ref, *refs):
    out_ref = refs[-1]
    line, _, _, width, _ = out_ref.shape
    for which, ref in enumerate(refs[:-1]):
        for target in range(line):
            for half in range(2):
                first = (half * line + target) * width
                out_ref[target, which, half] = ref[:, first : first + width].T


def pack_weights(after, weights, line):
    height, columns = weights[0].shape
    out = (line, len(weights), 2, columns // (2 * line), height)
    return pl.pallas_call(
        pack_kernel,
        out_shape=jax.ShapeDtypeStruct(out, weights[0].dtype),
        in_specs=[ANY] + [VMEM] * len(weights),
        out_specs=VMEM,
        compiler_params=PARAMS,
        cost_estimate=pl.CostEstimate(
            flops=0, bytes_accessed=4 * height * columns * len(weights), transcendentals=0
        ),
    )(after, *weights)


def scale_kernel(height, pick_ref, gain_ref, *refs):
    arrays, out_ref = refs[:-1], refs[-1]
    parts = out_ref.shape[0]
    tall = height + EXTRA
    blocks = [
        ref.at[first : first + tall] for ref in arrays for first in range(0, ref.shape[0], tall)
    ]
    each = len(blocks) // parts
    count = out_ref.shape[2] // each
    slots = each // 2 if each > 1 else 1
    features = 2 * height * parts
    gain_columns = gain_ref[...].T
    for number in range(each):
        slot, half = number % slots, number // slots
        first = (slot * (each // slots) + half) * count
        squares = jnp.zeros((1, count), jnp.float32)
        for block in blocks[number::each]:
            terms = block[height:tall, :].astype(jnp.float32)
            squares += jnp.sum(terms, axis=0, keepdims=True)
        inv_row = lax.rsqrt(squares / features + epsilon)
        for part in range(parts):
            scaled = blocks[part * each + number][0:height, :].astype(jnp.float32) * inv_row
            scaled = (scaled * gain_columns[:, part : part + 1]).astype(jnp.bfloat16)
            out_ref[pick_ref[part], :, first : first + count] = scaled


def scale(picks, gains, height, arrays):
    parts = picks.shape[0]
    count = arrays[0].shape[1]
    each = sum(array.shape[0] for array in arrays) // (height + EXTRA) // parts
    return pl.pallas_call(
        functools.partial(scale_kernel, height),
        out_shape=jax.ShapeDtypeStruct((parts, height, count * each), jnp.bfloat16),
        in_specs=[SMEM] + [VMEM] * (1 + len(arrays)),
        out_specs=VMEM,
        compiler_params=PARAMS,
        cost_estimate=pl.CostEstimate(
            flops=2 * parts * height * count * each,
            bytes_accessed=4 * parts * height * count * each,
            transcendentals=0,
        ),
    )(picks, gains, *arrays)


def project_kernel(number, row_count, x_ref, weight_ref, *refs):
    mine_ref, other_ref = refs[-2:]
    x = x_ref[0]
    first = 0
    for ref in refs[:-2]:
        parts, _, count = ref.shape
        mine = jnp.zeros((mine_ref.shape[0], count), jnp.float32)
        other = jnp.zeros((mine_ref.shape[0], count), jnp.float32)
        for part in range(parts):
            block = ref[part]
            mine += jnp.dot(
                weight_ref[part, number, x], block, preferred_element_type=jnp.float32
            )
            other += jnp.dot(
                weight_ref[part, number, 1 - x], block, preferred_element_type=jnp.float32
            )
        mine_ref[:, first : first + count] = mine
        other = other.astype(jnp.bfloat16)
        other_ref[:, first : first + row_count] = other[:, row_count:]
        other_ref[:, first + row_count : first + count] = other[:, :row_count]
        first += count


def project(x, weights, number, normed, row_count):
    line, _, _, width, height = weights.shape
    out = (width, sum(some.shape[2] for some in normed))
    return pl.pallas_call(
        functools.partial(project_kernel, number, row_count),
        out_shape=[
            jax.ShapeDtypeStruct(out, jnp.float32),
            jax.ShapeDtypeStruct(out, jnp.bfloat16),
        ],
        in_specs=[SMEM] + [VMEM] * (1 + len(normed)),
        out_specs=[VMEM, VMEM],
        compiler_params=PARAMS,
        cost_estimate=pl.CostEstimate(
            flops=4 * width * height * out[1] * line,
            bytes_accessed=weights.size + 2 * height * out[1] * line,
            transcendentals=0,
        ),
    )(x, weights, *normed)


def column_of(row):
    tall = jnp.broadcast_to(row.astype(jnp.float32), (SUBLANES, row.shape[1])).T
    return tall[:, 0:1].astype(row.dtype)


def at_places(array, place_row, total):
    spot = lax.broadcasted_iota(jnp.int32, (array.shape[1], total), 1)
    onehot = (column_of(place_row) == spot).astype(jnp.float32).astype(jnp.bfloat16)
    return jnp.dot(array, onehot, preferred_element_type=jnp.float32)


def with_tokens(first, tall, summed, token_refs):
    chan = summed.shape[0]
    first = pl.multiple_of(first, chan)
    tokens = []
    for kept_ref, got_ref in zip(token_refs[::2], token_refs[1::2]):
        for start in range(0, kept_ref.shape[0], tall):
            tokens += [ref[pl.ds(first + start, chan), :] for ref in (kept_ref, got_ref)]
    return jnp.concatenate([summed, jnp.concatenate(tokens, axis=1)], axis=0)


def place_kernel(tall, many, first_ref, mine_ref, theirs_ref, place_ref, *refs):
    tokens, before, out_ref = refs[:many], refs[many:-1], refs[-1]
    count = place_ref.shape[1]
    summed = mine_ref[:, :count] + theirs_ref[:, :count].astype(jnp.float32)
    summed = summed.astype(jnp.bfloat16)
    if tokens:
        summed = with_tokens(first_ref[0], tall, summed, tokens)
    moved = at_places(summed, place_ref[...], out_ref.shape[1])
    for ref in before:
        moved += ref[...].astype(jnp.float32)
    out_ref[...] = moved.astype(jnp.bfloat16)


def place(first, total, mine, theirs, places, tall=0, tokens=(), before=()):
    chan, count = mine.shape[0], places.shape[1]
    return pl.pallas_call(
        functools.partial(place_kernel, tall, len(tokens)),
        out_shape=jax.ShapeDtypeStruct((2 * chan if tokens else chan, total), jnp.bfloat16),
        in_specs=[SMEM] + [VMEM] * (3 + len(tokens) + len(before)),
        out_specs=VMEM,
        compiler_params=PARAMS,
        cost_estimate=pl.CostEstimate(
            flops=2 * chan * total * count, bytes_accessed=8 * chan * total, transcendentals=0
        ),
    )(first, mine, theirs, places, *tokens, *before)


def band_kernel(
    taps_blocks, tall, flag_ref, first_ref, taps_ref, skip_ref, early_ref, mine_ref, theirs_ref,
    last_mine_ref, last_theirs_ref, place_ref, *refs
):
    shifted = refs[-taps_blocks - 1 :]
    out_ref, packed_ref, whole, band = refs[-taps_blocks - 5 : -taps_blocks - 1]
    chan = taps_ref.shape[0]
    total = whole.shape[1]
    pieces = total // LANES
    summed = jnp.concatenate(
        [
            (mine[...] + theirs[...].astype(jnp.float32)).astype(jnp.bfloat16)
            for mine, theirs in ((mine_ref, theirs_ref), (last_mine_ref, last_theirs_ref))
        ],
        axis=1,
    )
    summed = with_tokens(first_ref[0], tall, summed, refs[: -taps_blocks - 5])
    moved = at_places(summed, place_ref[...], total) + early_ref[...].astype(jnp.float32)
    whole[...] = moved[0:chan]
    packed_ref[...] = moved[chan : 2 * chan].astype(jnp.bfloat16)
    for piece in range(pieces):
        for back in range(taps_blocks + 1):
            rows = pl.ds(piece * chan, chan)
            if back > piece:
                shifted[back][rows, :] = jnp.zeros((chan, LANES), jnp.float32)
                continue
            first = (piece - back) * LANES
            part = whole[:, first : first + LANES]
            if back > piece % taps_blocks:
                part = part * flag_ref[piece // taps_blocks]
            shifted[back][rows, :] = part
    column = lax.broadcasted_iota(jnp.int32, (LANES, LANES), 1).astype(jnp.bfloat16)
    row = lax.broadcasted_iota(jnp.int32, (LANES, LANES), 0).astype(jnp.bfloat16)
    later = column >= row
    zero = jnp.zeros((LANES, LANES), jnp.bfloat16)

    def one(group, carry):
        base = pl.multiple_of(group * SUBLANES, SUBLANES)
        group_taps = taps_ref[pl.ds(base, SUBLANES), :]
        for member in range(SUBLANES):
            turned = [zero]
            for block in range(taps_blocks):
                line_row = group_taps[member : member + 1, block * LANES : (block + 1) * LANES]
                square = jnp.broadcast_to(line_row, (LANES, LANES))
                square = pltpu.roll(square, 0, 1, stride=1, stride_axis=0)
                turned.append(square.astype(jnp.bfloat16))
            turned.append(zero)
            rows = pl.ds(base + member, pieces, stride=chan)
            tiles, inputs = [], []
            for back in range(taps_blocks + 1):
                tiles.append(jnp.where(later, turned[back + 1], turned[back]))
                inputs.append(shifted[back][rows, :].astype(jnp.bfloat16))
            band[rows, :] = jnp.dot(
                jnp.concatenate(inputs, axis=1),
                jnp.concatenate(tiles, axis=0),
                preferred_element_type=jnp.float32,
            )
        return carry

    lax.fori_loop(0, chan // SUBLANES, one, 0, unroll=4)
    skip = column_of(skip_ref[...])
    for piece in range(pieces):
        lanes = slice(piece * LANES, (piece + 1) * LANES)
        rows = pl.ds(piece * chan, chan)
        out_ref[:, lanes] = (band[rows, :] + skip * whole[:, lanes]).astype(jnp.bfloat16)


def band_of(flags, first, taps, skip, early, late, last, places, tall, tokens):
    chan, tap_count = taps.shape
    total = early.shape[1]
    taps_blocks = tap_count // LANES
    tower = (total // LANES * chan, LANES)
    out = jax.ShapeDtypeStruct((chan, total), jnp.bfloat16)
    return pl.pallas_call(
        functools.partial(band_kernel, taps_blocks, tall),
        out_shape=[out, out],
        in_specs=[SMEM, SMEM] + [VMEM] * (8 + len(tokens)),
        out_specs=[VMEM, VMEM],
        scratch_shapes=[pltpu.VMEM((chan, total), jnp.float32)]
        + [pltpu.VMEM(tower, jnp.float32)] * (taps_blocks + 2),
        compiler_params=PARAMS,
        cost_estimate=pl.CostEstimate(
            flops=3 * chan * total * total, bytes_accessed=16 * chan * total, transcendentals=0
        ),
    )(flags, first, taps, skip, early, *late, *last, places, *tokens)


def mix_kernel(z_ref, packed_ref, early_ref, mine_ref, theirs_ref, place_ref, out_ref):
    summed = (mine_ref[...] + theirs_ref[...].astype(jnp.float32)).astype(jnp.bfloat16)
    gate = at_places(summed, place_ref[...], z_ref.shape[1]) + early_ref[...].astype(jnp.float32)
    mixed = packed_ref[...].astype(jnp.float32) + gate * z_ref[...].astype(jnp.float32)
    mixed = mixed.astype(jnp.bfloat16)
    wide = out_ref.shape[2]
    pairs = out_ref.shape[0] // 2
    for place in range(2 * pairs):
        owner = place % pairs * 2 + place // pairs
        out_ref[place] = mixed[:, owner * wide : (owner + 1) * wide]


def mix(z, packed, early, mine, theirs, places, shards):
    chan, total = z.shape
    return pl.pallas_call(
        mix_kernel,
        out_shape=jax.ShapeDtypeStruct((shards, chan, total // shards), jnp.bfloat16),
        in_specs=[VMEM] * 6,
        out_specs=VMEM,
        compiler_params=PARAMS,
        cost_estimate=pl.CostEstimate(
            flops=chan * total * total, bytes_accessed=16 * chan * total, transcendentals=0
        ),
    )(z, packed, early, mine, theirs, places)


def on_device_line(tokens, packing, norm_gain, w_value, w_gate, filters, skip_gain, lengths):
    shards, groups = lax.axis_size("seq"), lax.axis_size("mp")
    line = shards // 2
    s, m = lax.axis_index("seq"), lax.axis_index("mp")
    z, x = s // 2, s % 2
    features, row_count = tokens.shape
    half = features // 2
    total_rows = packing.shape[0]
    width = features // shards

    def number(zz, xx, mm):
        return (zz * 2 + xx) * groups + mm

    def send(array, target):
        pairs = []
        for zz in range(line):
            for xx in range(2):
                for mm in range(groups):
                    to = target(zz, xx, mm)
                    if to is not None:
                        pairs.append((number(zz, xx, mm), number(*to)))
        return lax.ppermute(array, AXES, pairs)

    def across(array):
        return send(array, lambda zz, xx, mm: (zz, 1 - xx, mm))

    def to_owner(array, o):
        return send(array, lambda zz, xx, mm: (zz, xx, mm ^ o))

    columns = [[number(zz, xx, mm) for zz in range(line)] for xx in range(2) for mm in range(groups)]

    def along_line(array):
        return lax.all_to_all(
            array, AXES, split_axis=0, concat_axis=0, tiled=True, axis_index_groups=columns
        )

    def to_pair(array, o):
        return send(array, lambda zz, xx, mm: (zz ^ o, xx, mm))

    slot_pair = jnp.stack([z ^ o for o in range(line)])
    far_owner, near_owner, far_pair, near_pair = groups // 2, groups // 4, line // 2, line // 4
    owners = jnp.stack([m ^ o for o in (0, far_owner, near_owner, far_owner ^ near_owner)])
    which = x[None].astype(jnp.int32)
    picks = owners.astype(jnp.int32)
    gains = norm_gain.reshape(groups, 2, half)[:, x][owners]
    gains = jnp.pad(gains, ((0, -groups % SUBLANES), (0, 0)))
    places = packing.reshape(line, 2, row_count)[slot_pair]
    places = jnp.stack([places[:, x], places[:, 1 - x]], axis=1).reshape(1, total_rows)
    first = x * half + z * width
    taps = lax.dynamic_slice_in_dim(filters, first, width, 0).astype(jnp.float32)
    skip = lax.dynamic_slice_in_dim(skip_gain, first, width, 0)[None]
    flags = doc_flags(lengths, total_rows // filters.shape[1], jnp.float32)
    row_first = (z * width)[None].astype(jnp.int32)
    tall = half + EXTRA
    wide = 2 * row_count

    def projected(number, some):
        return project(which, weights, number, some, row_count)

    def scaled(arrays):
        return scale(picks, gains, half, arrays)

    def to_near(arrays):
        stacked = jnp.concatenate(arrays, axis=0) if len(arrays) > 1 else arrays[0]
        return to_owner(stacked, near_owner)

    def tie(*arrays):
        return lax.optimization_barrier(arrays)

    by_far, by_near = to_pair(tokens, far_pair), to_pair(tokens, near_pair)
    kept0, give0 = halve(which, tokens)
    got0, kept0_far = across(give0), to_owner(kept0, far_owner)
    got0_far = to_owner(got0, far_owner)
    most0 = jnp.concatenate([kept0, got0, kept0_far, got0_far], axis=0)
    packed_weights = pack_weights(give0, [w_value, w_gate], line)
    packed_weights, by_near, most0 = tie(packed_weights, by_near, most0)
    kept1, give1 = halve(which, by_near)
    small = picks, gains, taps, skip, flags, row_first, places, which
    by_both = to_pair(by_far, near_pair)
    by_far, got0, kept0_far, got0_far, most0, kept1, give1, small, packed_weights = tie(
        by_far, got0, kept0_far, got0_far, most0, kept1, give1, small, packed_weights
    )
    picks, gains, taps, skip, flags, row_first, places, which = small

    kept2, give2 = halve(which, by_far)
    got1, kept1_far = across(give1), to_owner(kept1, far_owner)
    got2, kept2_far = across(give2), to_owner(kept2, far_owner)
    got1_far = to_owner(got1, far_owner)
    weights = along_line(packed_weights)
    got2_far = to_owner(got2, far_owner)
    by_both, got1, kept1_far, got1_far, got2, kept2_far = tie(
        by_both, got1, kept1_far, got1_far, got2, kept2_far
    )

    kept3, give3 = halve(which, by_both)
    got3, kept3_far = across(give3), to_owner(kept3, far_owner)
    all1 = to_near([kept1, got1, kept1_far, got1_far])
    all0 = to_near([most0])
    got3, kept3_far, got2_far, all0, all1 = tie(got3, kept3_far, got2_far, all0, all1)

    got3_far = to_owner(got3, far_owner)
    all2 = to_near([kept2, got2, kept2_far, got2_far])
    near_kept3, near_kept3_far, near_got3 = [to_near([some]) for some in (kept3, kept3_far, got3)]
    normed0 = scaled([kept0, got0, kept0_far, got0_far, all0])
    normed1 = scaled([kept1, got1, kept1_far, got1_far, all1])
    got3_far, all2, near_kept3, near_kept3_far, near_got3, normed0, normed1 = tie(
        got3_far, all2, near_kept3, near_kept3_far, near_got3, normed0, normed1
    )

    near_got3_far = to_near([got3_far])
    normed2 = scaled([kept2, got2, kept2_far, got2_far, all2])
    near_got3_far, normed2 = tie(near_got3_far, normed2)
    normed3 = scaled(
        [kept3, got3, kept3_far, got3_far, near_kept3, near_got3, near_kept3_far, near_got3_far]
    )
    normed3, weights = tie(normed3, weights)

    value0, far0 = projected(0, [normed0])
    theirs0 = across(far0)
    value0, normed1 = tie(value0, normed1)
    value1, far1 = projected(0, [normed1, normed2])
    theirs1 = across(far1)
    value1, normed3, theirs0 = tie(value1, normed3, theirs0)
    value3, far3 = projected(0, [normed3])
    theirs3 = across(far3)
    normed0, normed3, value3 = tie(normed0, normed3, value3)
    gate0, gate_far0 = projected(1, [normed0, normed1])
    gate2, gate_far2 = projected(1, [normed2, normed3])
    early = place(
        row_first, total_rows, value0, theirs0, places[:, :wide], tall, [kept0, got0]
    )
    theirs1, gate_far0, gate_far2 = tie(theirs1, gate_far0, gate_far2)
    gate_theirs0, gate_theirs2 = across(gate_far0), across(gate_far2)
    banded, packed = band_of(
        flags, row_first, taps, skip, early, (value1, theirs1), (value3, theirs3),
        places[:, wide:], tall, [kept1, got1, kept2, got2, kept3, got3],
    )
    cut = 2 * wide
    early = place(row_first, total_rows, gate0, gate_theirs0, places[:, :cut])
    mixed = mix(banded, packed, early, gate2, gate_theirs2, places[:, cut:], shards)
    owners = [[number(zz, xx, mm) for xx in range(2) for zz in range(line)] for mm in range(groups)]
    mixed = lax.all_to_all(
        mixed, AXES, split_axis=0, concat_axis=0, tiled=True, axis_index_groups=owners
    )
    return mixed.reshape(features, row_count)


def solution(mesh):
    placed = (P("mp", "seq"), P(), P(), P("seq", "mp"), P("seq", "mp"), P("mp", None), P("mp"), P())
    shards, groups = mesh.shape["seq"], mesh.shape["mp"]

    def whole(*args):
        tokens, w_value, filters = args[0], args[3], args[5]
        moves_tokens = (
            tokens.shape[1] <= w_value.shape[1]
            and shards == 2 * groups
            and groups & (groups - 1) == 0
            and (groups - 1).bit_count() == 2
            and tokens.shape[0] % (LANES * shards * groups) == 0
            and filters.shape[1] % LANES == 0
            and tokens.shape[1] // shards % filters.shape[1] == 0
        )
        body = on_device_line if moves_tokens else on_device
        return jax.shard_map(
            body, mesh=mesh, in_specs=placed, out_specs=P("mp", "seq"), check_vma=False
        )(*args)

    return whole
```

```python
import functools
import math

import jax
import jax.numpy as jnp
from jax import lax
from jax.experimental import pallas as pl
from jax.experimental.pallas import tpu as pltpu
from jax.sharding import PartitionSpec as P

epsilon = 1e-05
AXES = ("seq", "mp")
LANES = 128
SUBLANES = 8
EXTRA = 2 * SUBLANES
VMEM = pl.BlockSpec(memory_space=pltpu.VMEM)
ANY = pl.BlockSpec(memory_space=pl.ANY)
SMEM = pl.BlockSpec(memory_space=pltpu.SMEM)
PARAMS = pltpu.CompilerParams(vmem_limit_bytes=16 * 1024 * 1024)


def toeplitz(filter_taps):
    chan_count, tap_count = filter_taps.shape
    padding = jnp.zeros((chan_count, tap_count), filter_taps.dtype)
    line_row = jnp.concatenate([padding, filter_taps[:, ::-1], padding], axis=1)
    tiled = jnp.tile(line_row, (1, tap_count))[:, : tap_count * (3 * tap_count - 1)]
    return tiled.reshape(chan_count, tap_count, 3 * tap_count - 1)[
        :, :, tap_count - 1 : 3 * tap_count - 1
    ]


def doc_flags(lengths, block_count, dtype):
    starts = jnp.cumsum(lengths, dtype=jnp.int32) - lengths
    block_index = jnp.arange(block_count, dtype=jnp.int32)
    is_start = jnp.any(block_index[:, None] == starts[None, :], axis=1)
    return jnp.where(is_start, 0.0, 1.0).astype(dtype)


def band_product(values, prior_rim, filter_taps, link_flags):
    chan_count, seq_length = values.shape
    tap_count = filter_taps.shape[1]
    block_count = seq_length // tap_count
    group_size = math.gcd(chan_count, 64)
    groups = chan_count // group_size

    def one_group(group_args):
        part_values, part_rim, part_taps = group_args
        blocks = part_values.reshape(group_size, block_count, tap_count)
        earlier = jnp.concatenate([part_rim[:, None, :], blocks[:, :-1, :]], axis=1)
        earlier = earlier * link_flags[None, :, None]
        joined = jnp.concatenate([earlier, blocks], axis=2)
        banded = jnp.einsum(
            "cpq,cbq->cbp", toeplitz(part_taps), joined, preferred_element_type=jnp.float32
        )
        return banded.reshape(group_size, seq_length)

    result = lax.map(
        one_group,
        (
            values.reshape(groups, group_size, seq_length),
            prior_rim.reshape(groups, group_size, tap_count),
            filter_taps.reshape(groups, group_size, tap_count),
        ),
    )
    return result.reshape(chan_count, seq_length)


def project_all(all_features, norm_gain, weight_pair):
    widened = all_features.astype(jnp.float32)
    inv_scale = lax.rsqrt(jnp.mean(widened * widened, axis=0, keepdims=True) + epsilon)
    normed = (widened * inv_scale * norm_gain[:, None]).astype(jnp.bfloat16)
    contract = (((0,), (0,)), ((), ()))
    value_part = lax.dot_general(
        weight_pair[0], normed, contract, preferred_element_type=jnp.float32
    ).astype(jnp.bfloat16)
    gate_part = lax.dot_general(
        weight_pair[1], normed, contract, preferred_element_type=jnp.float32
    ).astype(jnp.bfloat16)
    return (value_part, gate_part)


def on_device(tokens, packing, norm_gain, w_value, w_gate, filters, skip_gain, lengths):
    row_count = tokens.shape[1]
    shards = lax.axis_size("seq")
    my_index = lax.axis_index("seq")
    all_count = packing.shape[0]
    tap_count = filters.shape[1]
    chan_count = tokens.shape[0] // shards
    weight_pair = (
        lax.all_gather(w_value, "seq", axis=0, tiled=True),
        lax.all_gather(w_gate, "seq", axis=0, tiled=True),
    )
    inverse = (
        jnp.zeros((all_count,), jnp.int32).at[packing].set(jnp.arange(all_count, dtype=jnp.int32))
    )
    chan_taps = lax.dynamic_slice_in_dim(filters, my_index * chan_count, chan_count, 0)
    chan_skip = lax.dynamic_slice_in_dim(skip_gain, my_index * chan_count, chan_count, 0)
    slot_cap = 2 * (row_count // shards)
    own_packing = lax.dynamic_slice_in_dim(packing, my_index * row_count, row_count)
    dest_owner = own_packing // row_count
    onehot = (dest_owner[:, None] == jnp.arange(shards, dtype=jnp.int32)[None, :]).astype(jnp.int32)
    slot_rank = jnp.sum((jnp.cumsum(onehot, axis=0, dtype=jnp.int32) - onehot) * onehot, axis=1)
    slot_index = dest_owner * slot_cap + slot_rank
    send_buffer = (
        jnp.zeros((tokens.shape[0], shards * slot_cap), jnp.bfloat16).at[:, slot_index].set(tokens)
    )
    received = lax.all_to_all(send_buffer, "seq", split_axis=1, concat_axis=1, tiled=True)
    my_sources = lax.dynamic_slice_in_dim(inverse, my_index * row_count, row_count)
    to_me = (packing // row_count == my_index).astype(jnp.int32).reshape(shards, row_count)
    arrival_rank = (jnp.cumsum(to_me, axis=1, dtype=jnp.int32) - to_me).reshape(all_count)
    packed = received[:, my_sources // row_count * slot_cap + arrival_rank[my_sources]]
    all_features = lax.all_gather(packed, "mp", axis=0, tiled=True)
    value_part, gate_part = project_all(all_features, norm_gain, weight_pair)
    value_chan = lax.all_to_all(value_part, "seq", split_axis=0, concat_axis=1, tiled=True)
    link_flags = doc_flags(lengths, all_count // tap_count, jnp.bfloat16)
    prior_rim = jnp.zeros((chan_count, tap_count), jnp.bfloat16)
    banded = band_product(value_chan, prior_rim, chan_taps, link_flags)
    chan_band = (banded + chan_skip[:, None] * value_chan.astype(jnp.float32)).astype(jnp.bfloat16)
    mixed_band = lax.all_to_all(chan_band, "seq", split_axis=1, concat_axis=0, tiled=True)
    mixed_band = lax.optimization_barrier(mixed_band)
    gate_wide = lax.optimization_barrier(gate_part).astype(jnp.float32)
    return (packed.astype(jnp.float32) + gate_wide * mixed_band.astype(jnp.float32)).astype(
        jnp.bfloat16
    )


def halve_kernel(x_ref, token_ref, keep_ref, give_ref):
    features, count = token_ref.shape
    half = features // 2
    x = x_ref[0]
    widened = token_ref[...].astype(jnp.float32)
    rest = jnp.sum(widened * widened, axis=0, keepdims=True)
    terms = []
    for _ in range(3):
        term = rest.astype(jnp.bfloat16).astype(jnp.float32)
        terms.append(term)
        rest = rest - term
    row = lax.broadcasted_iota(jnp.int32, (EXTRA, count), 0)
    extra = jnp.zeros(row.shape, jnp.float32)
    for i, term in enumerate(terms):
        extra = jnp.where(row == i, term, extra)
    extra = extra.astype(jnp.bfloat16)
    for out_ref, which in ((keep_ref, x), (give_ref, 1 - x)):
        out_ref[0:half, :] = token_ref[pl.ds(pl.multiple_of(which * half, half), half), :]
        out_ref[half : half + EXTRA, :] = extra


def halve(x, tokens):
    features, count = tokens.shape
    out = jax.ShapeDtypeStruct((features // 2 + EXTRA, count), tokens.dtype)
    return pl.pallas_call(
        halve_kernel,
        out_shape=[out, out],
        in_specs=[SMEM, VMEM],
        out_specs=[VMEM, VMEM],
        compiler_params=PARAMS,
        cost_estimate=pl.CostEstimate(
            flops=2 * features * count, bytes_accessed=4 * features * count, transcendentals=0
        ),
    )(x, tokens)


def pack_kernel(after_ref, *refs):
    out_ref = refs[-1]
    line, _, _, width, _ = out_ref.shape
    for which, ref in enumerate(refs[:-1]):
        for target in range(line):
            for half in range(2):
                first = (half * line + target) * width
                out_ref[target, which, half] = ref[:, first : first + width].T


def pack_weights(after, weights, line):
    height, columns = weights[0].shape
    out = (line, len(weights), 2, columns // (2 * line), height)
    return pl.pallas_call(
        pack_kernel,
        out_shape=jax.ShapeDtypeStruct(out, weights[0].dtype),
        in_specs=[ANY] + [VMEM] * len(weights),
        out_specs=VMEM,
        compiler_params=PARAMS,
        cost_estimate=pl.CostEstimate(
            flops=0, bytes_accessed=4 * height * columns * len(weights), transcendentals=0
        ),
    )(after, *weights)


def scale_kernel(height, pick_ref, gain_ref, *refs):
    arrays, out_ref = refs[:-1], refs[-1]
    parts = out_ref.shape[0]
    tall = height + EXTRA
    blocks = [
        ref.at[first : first + tall] for ref in arrays for first in range(0, ref.shape[0], tall)
    ]
    each = len(blocks) // parts
    count = out_ref.shape[2] // each
    slots = each // 2 if each > 1 else 1
    features = 2 * height * parts
    gain_columns = gain_ref[...].T
    for number in range(each):
        slot, half = number % slots, number // slots
        first = (slot * (each // slots) + half) * count
        squares = jnp.zeros((1, count), jnp.float32)
        for block in blocks[number::each]:
            terms = block[height:tall, :].astype(jnp.float32)
            squares += jnp.sum(terms, axis=0, keepdims=True)
        inv_row = lax.rsqrt(squares / features + epsilon)
        for part in range(parts):
            scaled = blocks[part * each + number][0:height, :].astype(jnp.float32) * inv_row
            scaled = (scaled * gain_columns[:, part : part + 1]).astype(jnp.bfloat16)
            out_ref[pick_ref[part], :, first : first + count] = scaled


def scale(picks, gains, height, arrays):
    parts = picks.shape[0]
    count = arrays[0].shape[1]
    each = sum(array.shape[0] for array in arrays) // (height + EXTRA) // parts
    return pl.pallas_call(
        functools.partial(scale_kernel, height),
        out_shape=jax.ShapeDtypeStruct((parts, height, count * each), jnp.bfloat16),
        in_specs=[SMEM] + [VMEM] * (1 + len(arrays)),
        out_specs=VMEM,
        compiler_params=PARAMS,
        cost_estimate=pl.CostEstimate(
            flops=2 * parts * height * count * each,
            bytes_accessed=4 * parts * height * count * each,
            transcendentals=0,
        ),
    )(picks, gains, *arrays)


def project_kernel(number, row_count, x_ref, weight_ref, *refs):
    mine_ref, other_ref = refs[-2:]
    x = x_ref[0]
    first = 0
    for ref in refs[:-2]:
        parts, _, count = ref.shape
        mine = jnp.zeros((mine_ref.shape[0], count), jnp.float32)
        other = jnp.zeros((mine_ref.shape[0], count), jnp.float32)
        for part in range(parts):
            block = ref[part]
            mine += jnp.dot(
                weight_ref[part, number, x], block, preferred_element_type=jnp.float32
            )
            other += jnp.dot(
                weight_ref[part, number, 1 - x], block, preferred_element_type=jnp.float32
            )
        mine_ref[:, first : first + count] = mine
        other = other.astype(jnp.bfloat16)
        other_ref[:, first : first + row_count] = other[:, row_count:]
        other_ref[:, first + row_count : first + count] = other[:, :row_count]
        first += count


def project(x, weights, number, normed, row_count):
    line, _, _, width, height = weights.shape
    out = (width, sum(some.shape[2] for some in normed))
    return pl.pallas_call(
        functools.partial(project_kernel, number, row_count),
        out_shape=[
            jax.ShapeDtypeStruct(out, jnp.float32),
            jax.ShapeDtypeStruct(out, jnp.bfloat16),
        ],
        in_specs=[SMEM] + [VMEM] * (1 + len(normed)),
        out_specs=[VMEM, VMEM],
        compiler_params=PARAMS,
        cost_estimate=pl.CostEstimate(
            flops=4 * width * height * out[1] * line,
            bytes_accessed=weights.size + 2 * height * out[1] * line,
            transcendentals=0,
        ),
    )(x, weights, *normed)


def column_of(row):
    tall = jnp.broadcast_to(row.astype(jnp.float32), (SUBLANES, row.shape[1])).T
    return tall[:, 0:1].astype(row.dtype)


def at_places(array, place_row, total):
    spot = lax.broadcasted_iota(jnp.int32, (array.shape[1], total), 1)
    onehot = (column_of(place_row) == spot).astype(jnp.float32).astype(jnp.bfloat16)
    return jnp.dot(array, onehot, preferred_element_type=jnp.float32)


def with_tokens(first, tall, summed, token_refs):
    chan = summed.shape[0]
    first = pl.multiple_of(first, chan)
    tokens = []
    for kept_ref, got_ref in zip(token_refs[::2], token_refs[1::2]):
        for start in range(0, kept_ref.shape[0], tall):
            tokens += [ref[pl.ds(first + start, chan), :] for ref in (kept_ref, got_ref)]
    return jnp.concatenate([summed, jnp.concatenate(tokens, axis=1)], axis=0)


def place_kernel(tall, many, first_ref, mine_ref, theirs_ref, place_ref, *refs):
    tokens, before, out_ref = refs[:many], refs[many:-1], refs[-1]
    count = place_ref.shape[1]
    summed = mine_ref[:, :count] + theirs_ref[:, :count].astype(jnp.float32)
    summed = summed.astype(jnp.bfloat16)
    if tokens:
        summed = with_tokens(first_ref[0], tall, summed, tokens)
    moved = at_places(summed, place_ref[...], out_ref.shape[1])
    for ref in before:
        moved += ref[...].astype(jnp.float32)
    out_ref[...] = moved.astype(jnp.bfloat16)


def place(first, total, mine, theirs, places, tall=0, tokens=(), before=()):
    chan, count = mine.shape[0], places.shape[1]
    return pl.pallas_call(
        functools.partial(place_kernel, tall, len(tokens)),
        out_shape=jax.ShapeDtypeStruct((2 * chan if tokens else chan, total), jnp.bfloat16),
        in_specs=[SMEM] + [VMEM] * (3 + len(tokens) + len(before)),
        out_specs=VMEM,
        compiler_params=PARAMS,
        cost_estimate=pl.CostEstimate(
            flops=2 * chan * total * count, bytes_accessed=8 * chan * total, transcendentals=0
        ),
    )(first, mine, theirs, places, *tokens, *before)


def band_kernel(
    taps_blocks, tall, flag_ref, first_ref, taps_ref, skip_ref, early_ref, mine_ref, theirs_ref,
    last_mine_ref, last_theirs_ref, place_ref, *refs
):
    shifted = refs[-taps_blocks - 1 :]
    out_ref, packed_ref, whole, band = refs[-taps_blocks - 5 : -taps_blocks - 1]
    chan = taps_ref.shape[0]
    total = whole.shape[1]
    pieces = total // LANES
    summed = jnp.concatenate(
        [
            (mine[...] + theirs[...].astype(jnp.float32)).astype(jnp.bfloat16)
            for mine, theirs in ((mine_ref, theirs_ref), (last_mine_ref, last_theirs_ref))
        ],
        axis=1,
    )
    summed = with_tokens(first_ref[0], tall, summed, refs[: -taps_blocks - 5])
    moved = at_places(summed, place_ref[...], total) + early_ref[...].astype(jnp.float32)
    whole[...] = moved[0:chan]
    packed_ref[...] = moved[chan : 2 * chan].astype(jnp.bfloat16)
    for piece in range(pieces):
        for back in range(taps_blocks + 1):
            rows = pl.ds(piece * chan, chan)
            if back > piece:
                shifted[back][rows, :] = jnp.zeros((chan, LANES), jnp.float32)
                continue
            first = (piece - back) * LANES
            part = whole[:, first : first + LANES]
            if back > piece % taps_blocks:
                part = part * flag_ref[piece // taps_blocks]
            shifted[back][rows, :] = part
    column = lax.broadcasted_iota(jnp.int32, (LANES, LANES), 1).astype(jnp.bfloat16)
    row = lax.broadcasted_iota(jnp.int32, (LANES, LANES), 0).astype(jnp.bfloat16)
    later = column >= row
    zero = jnp.zeros((LANES, LANES), jnp.bfloat16)

    def one(group, carry):
        base = pl.multiple_of(group * SUBLANES, SUBLANES)
        group_taps = taps_ref[pl.ds(base, SUBLANES), :]
        for member in range(SUBLANES):
            turned = [zero]
            for block in range(taps_blocks):
                line_row = group_taps[member : member + 1, block * LANES : (block + 1) * LANES]
                square = jnp.broadcast_to(line_row, (LANES, LANES))
                square = pltpu.roll(square, 0, 1, stride=1, stride_axis=0)
                turned.append(square.astype(jnp.bfloat16))
            turned.append(zero)
            rows = pl.ds(base + member, pieces, stride=chan)
            tiles, inputs = [], []
            for back in range(taps_blocks + 1):
                tiles.append(jnp.where(later, turned[back + 1], turned[back]))
                inputs.append(shifted[back][rows, :].astype(jnp.bfloat16))
            band[rows, :] = jnp.dot(
                jnp.concatenate(inputs, axis=1),
                jnp.concatenate(tiles, axis=0),
                preferred_element_type=jnp.float32,
            )
        return carry

    lax.fori_loop(0, chan // SUBLANES, one, 0, unroll=4)
    skip = column_of(skip_ref[...])
    for piece in range(pieces):
        lanes = slice(piece * LANES, (piece + 1) * LANES)
        rows = pl.ds(piece * chan, chan)
        out_ref[:, lanes] = (band[rows, :] + skip * whole[:, lanes]).astype(jnp.bfloat16)


def band_of(flags, first, taps, skip, early, late, last, places, tall, tokens):
    chan, tap_count = taps.shape
    total = early.shape[1]
    taps_blocks = tap_count // LANES
    tower = (total // LANES * chan, LANES)
    out = jax.ShapeDtypeStruct((chan, total), jnp.bfloat16)
    return pl.pallas_call(
        functools.partial(band_kernel, taps_blocks, tall),
        out_shape=[out, out],
        in_specs=[SMEM, SMEM] + [VMEM] * (8 + len(tokens)),
        out_specs=[VMEM, VMEM],
        scratch_shapes=[pltpu.VMEM((chan, total), jnp.float32)]
        + [pltpu.VMEM(tower, jnp.float32)] * (taps_blocks + 2),
        compiler_params=PARAMS,
        cost_estimate=pl.CostEstimate(
            flops=3 * chan * total * total, bytes_accessed=16 * chan * total, transcendentals=0
        ),
    )(flags, first, taps, skip, early, *late, *last, places, *tokens)


def mix_kernel(z_ref, packed_ref, early_ref, mine_ref, theirs_ref, place_ref, out_ref):
    summed = (mine_ref[...] + theirs_ref[...].astype(jnp.float32)).astype(jnp.bfloat16)
    gate = at_places(summed, place_ref[...], z_ref.shape[1]) + early_ref[...].astype(jnp.float32)
    mixed = packed_ref[...].astype(jnp.float32) + gate * z_ref[...].astype(jnp.float32)
    mixed = mixed.astype(jnp.bfloat16)
    wide = out_ref.shape[2]
    pairs = out_ref.shape[0] // 2
    for place in range(2 * pairs):
        owner = place % pairs * 2 + place // pairs
        out_ref[place] = mixed[:, owner * wide : (owner + 1) * wide]


def mix(z, packed, early, mine, theirs, places, shards):
    chan, total = z.shape
    return pl.pallas_call(
        mix_kernel,
        out_shape=jax.ShapeDtypeStruct((shards, chan, total // shards), jnp.bfloat16),
        in_specs=[VMEM] * 6,
        out_specs=VMEM,
        compiler_params=PARAMS,
        cost_estimate=pl.CostEstimate(
            flops=chan * total * total, bytes_accessed=16 * chan * total, transcendentals=0
        ),
    )(z, packed, early, mine, theirs, places)


def on_device_line(tokens, packing, norm_gain, w_value, w_gate, filters, skip_gain, lengths):
    shards, groups = lax.axis_size("seq"), lax.axis_size("mp")
    line = shards // 2
    s, m = lax.axis_index("seq"), lax.axis_index("mp")
    z, x = s // 2, s % 2
    features, row_count = tokens.shape
    half = features // 2
    total_rows = packing.shape[0]
    width = features // shards

    def number(zz, xx, mm):
        return (zz * 2 + xx) * groups + mm

    def send(array, target):
        pairs = []
        for zz in range(line):
            for xx in range(2):
                for mm in range(groups):
                    to = target(zz, xx, mm)
                    if to is not None:
                        pairs.append((number(zz, xx, mm), number(*to)))
        return lax.ppermute(array, AXES, pairs)

    def across(array):
        return send(array, lambda zz, xx, mm: (zz, 1 - xx, mm))

    def to_owner(array, o):
        return send(array, lambda zz, xx, mm: (zz, xx, mm ^ o))

    columns = [[number(zz, xx, mm) for zz in range(line)] for xx in range(2) for mm in range(groups)]

    def along_line(array):
        return lax.all_to_all(
            array, AXES, split_axis=0, concat_axis=0, tiled=True, axis_index_groups=columns
        )

    def to_pair(array, o):
        return send(array, lambda zz, xx, mm: (zz ^ o, xx, mm))

    slot_pair = jnp.stack([z ^ o for o in range(line)])
    far_owner, near_owner, far_pair, near_pair = groups // 2, groups // 4, line // 2, line // 4
    owners = jnp.stack([m ^ o for o in (0, far_owner, near_owner, far_owner ^ near_owner)])
    which = x[None].astype(jnp.int32)
    picks = owners.astype(jnp.int32)
    gains = norm_gain.reshape(groups, 2, half)[:, x][owners]
    gains = jnp.pad(gains, ((0, -groups % SUBLANES), (0, 0)))
    places = packing.reshape(line, 2, row_count)[slot_pair]
    places = jnp.stack([places[:, x], places[:, 1 - x]], axis=1).reshape(1, total_rows)
    first = x * half + z * width
    taps = lax.dynamic_slice_in_dim(filters, first, width, 0).astype(jnp.float32)
    skip = lax.dynamic_slice_in_dim(skip_gain, first, width, 0)[None]
    flags = doc_flags(lengths, total_rows // filters.shape[1], jnp.float32)
    row_first = (z * width)[None].astype(jnp.int32)
    tall = half + EXTRA
    wide = 2 * row_count

    def projected(number, some):
        return project(which, weights, number, some, row_count)

    def scaled(arrays):
        return scale(picks, gains, half, arrays)

    def to_near(arrays):
        stacked = jnp.concatenate(arrays, axis=0) if len(arrays) > 1 else arrays[0]
        return to_owner(stacked, near_owner)

    def tie(*arrays):
        return lax.optimization_barrier(arrays)

    by_far, by_near = to_pair(tokens, far_pair), to_pair(tokens, near_pair)
    kept0, give0 = halve(which, tokens)
    got0, kept0_far = across(give0), to_owner(kept0, far_owner)
    got0_far = to_owner(got0, far_owner)
    most0 = jnp.concatenate([kept0, got0, kept0_far, got0_far], axis=0)
    packed_weights = pack_weights(give0, [w_value, w_gate], line)
    packed_weights, by_near, most0 = tie(packed_weights, by_near, most0)
    kept1, give1 = halve(which, by_near)
    small = picks, gains, taps, skip, flags, row_first, places, which
    by_both = to_pair(by_far, near_pair)
    by_far, got0, kept0_far, got0_far, most0, kept1, give1, small, packed_weights = tie(
        by_far, got0, kept0_far, got0_far, most0, kept1, give1, small, packed_weights
    )
    picks, gains, taps, skip, flags, row_first, places, which = small

    kept2, give2 = halve(which, by_far)
    got1, kept1_far = across(give1), to_owner(kept1, far_owner)
    got2, kept2_far = across(give2), to_owner(kept2, far_owner)
    got1_far = to_owner(got1, far_owner)
    weights = along_line(packed_weights)
    got2_far = to_owner(got2, far_owner)
    by_both, got1, kept1_far, got1_far, got2, kept2_far = tie(
        by_both, got1, kept1_far, got1_far, got2, kept2_far
    )

    kept3, give3 = halve(which, by_both)
    got3, kept3_far = across(give3), to_owner(kept3, far_owner)
    all1 = to_near([kept1, got1, kept1_far, got1_far])
    all0 = to_near([most0])
    got3_far = to_owner(got3, far_owner)
    got3, kept3_far, got2_far, all0, all1 = tie(got3, kept3_far, got2_far, all0, all1)

    all2 = to_near([kept2, got2, kept2_far, got2_far])
    near_kept3, near_kept3_far, near_got3 = [to_near([some]) for some in (kept3, kept3_far, got3)]
    normed0 = scaled([kept0, got0, kept0_far, got0_far, all0])
    normed1 = scaled([kept1, got1, kept1_far, got1_far, all1])
    got3_far, all2, near_kept3, near_kept3_far, near_got3, normed0, normed1 = tie(
        got3_far, all2, near_kept3, near_kept3_far, near_got3, normed0, normed1
    )

    near_got3_far = to_near([got3_far])
    normed2 = scaled([kept2, got2, kept2_far, got2_far, all2])
    near_got3_far, normed2 = tie(near_got3_far, normed2)
    normed3 = scaled(
        [kept3, got3, kept3_far, got3_far, near_kept3, near_got3, near_kept3_far, near_got3_far]
    )
    normed3, weights = tie(normed3, weights)

    value0, far0 = projected(0, [normed0])
    theirs0 = across(far0)
    value0, normed1 = tie(value0, normed1)
    value1, far1 = projected(0, [normed1, normed2])
    theirs1 = across(far1)
    value1, normed3, theirs0 = tie(value1, normed3, theirs0)
    value3, far3 = projected(0, [normed3])
    theirs3 = across(far3)
    normed0, normed3, value3 = tie(normed0, normed3, value3)
    gate0, gate_far0 = projected(1, [normed0, normed1])
    gate2, gate_far2 = projected(1, [normed2, normed3])
    early = place(
        row_first, total_rows, value0, theirs0, places[:, :wide], tall, [kept0, got0]
    )
    theirs1, early, gate_far0, gate_far2 = tie(theirs1, early, gate_far0, gate_far2)
    gate_theirs0, gate_theirs2 = across(gate_far0), across(gate_far2)
    banded, packed = band_of(
        flags, row_first, taps, skip, early, (value1, theirs1), (value3, theirs3),
        places[:, wide:], tall, [kept1, got1, kept2, got2, kept3, got3],
    )
    cut = 2 * wide
    early = place(row_first, total_rows, gate0, gate_theirs0, places[:, :cut])
    mixed = mix(banded, packed, early, gate2, gate_theirs2, places[:, cut:], shards)
    owners = [[number(zz, xx, mm) for xx in range(2) for zz in range(line)] for mm in range(groups)]
    mixed = lax.all_to_all(
        mixed, AXES, split_axis=0, concat_axis=0, tiled=True, axis_index_groups=owners
    )
    return mixed.reshape(features, row_count)


def solution(mesh):
    placed = (P("mp", "seq"), P(), P(), P("seq", "mp"), P("seq", "mp"), P("mp", None), P("mp"), P())
    shards, groups = mesh.shape["seq"], mesh.shape["mp"]

    def whole(*args):
        tokens, w_value, filters = args[0], args[3], args[5]
        moves_tokens = (
            tokens.shape[1] <= w_value.shape[1]
            and shards == 2 * groups
            and groups & (groups - 1) == 0
            and (groups - 1).bit_count() == 2
            and tokens.shape[0] % (LANES * shards * groups) == 0
            and filters.shape[1] % LANES == 0
            and tokens.shape[1] // shards % filters.shape[1] == 0
        )
        body = on_device_line if moves_tokens else on_device
        return jax.shard_map(
            body, mesh=mesh, in_specs=placed, out_specs=P("mp", "seq"), check_vma=False
        )(*args)

    return whole
```
